32 devices in a mesh: grp: 2 (over y), gx: 4 (over z), gy: 2 (over core), shot: 2 (over x).
Axes of the slice: x: 2, y: 2, z: 4, core: 2. Of those that a mesh axis runs over, the one named last changes fastest.
Arguments:
- courant_sq: float32 [128, 64, 256], P('grp', 'gx', 'gy'), parts along dimension 0, may hold values from 0.02 to 0.2
- pressure_start: float32 [4, 64, 64, 256], P(('grp', 'shot'), None, 'gx', 'gy'), parts along dimension 0, may hold values from -6 to 6
- previous_start: float32 [4, 64, 64, 256], P(('grp', 'shot'), None, 'gx', 'gy'), parts along dimension 0, may hold values from -6 to 6
- wavelets: float32 [32, 20], P(('grp', 'shot')), parts along dimension 0, may hold values from -6 to 6
- traces: float32 [32, 20, 64, 256], P(('grp', 'shot'), None, 'gx', 'gy'), parts along dimension 0, may hold values from -1.5 to 1.5
- code_bits: int32 [32], P(('grp', 'shot')), parts along dimension 0, may hold values from 0 to 1
- assign: int32 [32], P(('grp', 'shot')), parts along dimension 0, may hold values from 0 to 1, as said below
- pos_x: int32 [32], P(('grp', 'shot')), parts along dimension 0, may hold values from 0 to 63
- pos_y: int32 [32], P(('grp', 'shot')), parts along dimension 0, may hold values from 0 to 255
Outputs:
- pressure: float32 [4, 64, 64, 256], P(('grp', 'shot'), None, 'gx', 'gy'), parts along dimension 0
- misfit: float32 [4, 20, 64, 256], P(('grp', 'shot'), None, 'gx', 'gy'), parts along dimension 0
The draws below stay inside these ranges and needn't reach their ends.
There are 2 independent parts, one for each index of `grp`. The reference program is written for one: setup_inputs(seed, part) draws one part's arguments, and reference() takes and returns one part's arrays. A program takes and returns all parts, laid end to end along the dimension named above; each array names one. Nothing has to cross between parts.
Inputs may be any that keep to these rules, and one draw needn't show every extreme that they name: `assign`: each supershot is the supershot of exactly 8 shots.
All inputs are finite; a program needn't handle non-finite values.
Results may differ from the reference program's by a relative error of at most 0.00027.
Values sent between devices are 32-bit elements; how exact they have to be, the bound alone decides.
A program may use at most 64 MiB of HBM per device.

```python
import jax
import jax.numpy as jnp
from jax import lax

NZ = 64
STEPS = 20
NX = 64
NY = 256
SHOTS = 16
NSUP = 2


def draw_code_bits(key, part):
    key = jax.random.fold_in(key, 23)
    return jax.random.randint(key, (SHOTS,), 0, 2, dtype=jnp.int32)


def draw_assign(key, part):
    key = jax.random.fold_in(key, 11)
    order = jax.random.permutation(key, jnp.arange(SHOTS, dtype=jnp.int32))
    return (order % NSUP).astype(jnp.int32)


def set_ends(result, key, low, top_value):
    spot = [jax.random.randint(jax.random.fold_in(key, axis), (), 0, length) for axis, length in enumerate(result.shape)]
    widest = result.shape.index(max(result.shape))
    neighbour = spot[:widest] + [(spot[widest] + 1) % result.shape[widest]] + spot[widest + 1:]
    return result.at[tuple(spot)].set(low).at[tuple(neighbour)].set(top_value)


def block_levels(stream_key, shape, pieces, low, high):
    gain = 1.0
    for dim, blocks in pieces:
        heights = jax.random.uniform(jax.random.fold_in(jax.random.fold_in(stream_key, 6), dim), (blocks,), jnp.float32, low / len(pieces), high / len(pieces))
        gain = gain * jnp.repeat(jnp.exp(heights), shape[dim] // blocks).reshape((-1,) + (1,) * (len(shape) - 1 - dim))
    return gain


def noise(stream_key, shape, width, most, pieces=(), held_as=jnp.bfloat16):
    factor_of = block_levels(stream_key, shape, pieces, -0.22, 0.18) if pieces else 1.0
    array = jax.random.normal(stream_key, shape, jnp.float32) * width * factor_of
    return jnp.minimum(jnp.maximum(array, -most), most).astype(held_as)


def setup_inputs(seed: int = 0, part: int = 0) -> dict:
    key_of = jax.random.split(jax.random.key(seed), 10)
    part_keys = jax.random.split(jax.random.fold_in(key_of[9], part), 10)
    return {
        "courant_sq": jnp.clip(0.02 + 0.18 * jax.random.uniform(part_keys[0], (NZ, NX, NY), jnp.float32) ** block_levels(part_keys[0], (NZ, NX, NY), ((1, 4), (2, 2)), -0.2, 0.2), 0.02, 0.2),
        "pressure_start": noise(part_keys[1], (NSUP, NZ, NX, NY), 1.0, 6.0, ((0, 2), (2, 4), (3, 2)), jnp.float32),
        "previous_start": noise(part_keys[2], (NSUP, NZ, NX, NY), 1.0, 6.0, ((0, 2), (2, 4), (3, 2)), jnp.float32),
        "wavelets": noise(part_keys[3], (SHOTS, STEPS), 1.0, 6.0, ((0, 2),), jnp.float32),
        "traces": noise(part_keys[4], (SHOTS, STEPS, NX, NY), 0.25, 1.5, ((0, 2), (2, 4), (3, 2)), jnp.float32),
        "code_bits": draw_code_bits(jax.random.fold_in(jax.random.fold_in(key_of[9], part), 71), part),
        "assign": draw_assign(jax.random.fold_in(jax.random.fold_in(key_of[9], part), 71), part),
        "pos_x": set_ends(jax.random.randint(part_keys[7], (SHOTS,), 0, NX), jax.random.fold_in(part_keys[7], 1), 0, NX - 1).astype(jnp.int32),
        "pos_y": set_ends(jax.random.randint(part_keys[8], (SHOTS,), 0, NY), jax.random.fold_in(part_keys[8], 1), 0, NY - 1).astype(jnp.int32),
    }


coeffs = (-205.0 / 72.0, 8.0 / 5.0, -1.0 / 5.0, 8.0 / 315.0, -1.0 / 560.0)
source_layer = 2
record_layer = 6


def laplace(field):
    depth, wide_x, wide_y = field.shape[1], field.shape[2], field.shape[3]
    padded = jnp.pad(field, ((0, 0), (4, 4), (4, 4), (4, 4)))

    def piece(dz, dx, dy):
        return padded[:, 4 + dz:4 + dz + depth, 4 + dx:4 + dx + wide_x, 4 + dy:4 + dy + wide_y]

    total = 3.0 * coeffs[0] * field
    for j in range(1, 5):
        total = total + coeffs[j] * (piece(j, 0, 0) + piece(-j, 0, 0))
        total = total + coeffs[j] * (piece(0, j, 0) + piece(0, -j, 0))
        total = total + coeffs[j] * (piece(0, 0, j) + piece(0, 0, -j))
    return total


def reference(courant_sq, pressure_start, previous_start, wavelets, traces, code_bits, assign, pos_x, pos_y):
    signs = (2 * code_bits - 1).astype(jnp.float32)
    encode = signs[:, None] * (assign[:, None] == jnp.arange(NSUP, dtype=jnp.int32)[None, :]).astype(jnp.float32)
    onex = (pos_x[:, None] == jnp.arange(NX, dtype=jnp.int32)[None, :]).astype(jnp.float32)
    oney = (pos_y[:, None] == jnp.arange(NY, dtype=jnp.int32)[None, :]).astype(jnp.float32)
    weighted = encode[:, :, None] * wavelets[:, None, :]
    place = onex[:, :, None] * oney[:, None, :]
    sources = jnp.einsum("skt,sxy->ktxy", weighted, place, precision=lax.Precision.HIGHEST)
    observed = jnp.einsum("sk,stxy->ktxy", encode, traces, precision=lax.Precision.HIGHEST)
    pressure = pressure_start
    previous = previous_start
    records = []
    for step in range(STEPS):
        nxt = 2.0 * pressure - previous + courant_sq[None] * laplace(pressure)
        nxt = nxt.at[:, source_layer].add(sources[:, step])
        records.append(nxt[:, record_layer] - observed[:, step])
        previous = pressure
        pressure = nxt
    return pressure, jnp.stack(records, axis=1)
```

```python
import functools

import jax
import jax.numpy as jnp
import ml_dtypes
from jax import lax
from jax.experimental import pallas as pl
from jax.experimental.pallas import tpu as pltpu
from jax.sharding import PartitionSpec as P

coeffs = (-205.0 / 72.0, 8.0 / 5.0, -1.0 / 5.0, 8.0 / 315.0, -1.0 / 560.0)
source_layer = 2
record_layer = 6
MESH = pl.DeviceIdType.MESH
HIGHEST = lax.Precision.HIGHEST
ROW = 8
CH = 8


def split_coeff(value):
    high = float(ml_dtypes.bfloat16(value))
    low = float(ml_dtypes.bfloat16(value - high))
    return high, low


def fill_band(ref, part):
    size = ref.shape[0]
    rows = lax.broadcasted_iota(jnp.int32, ref.shape, 0)
    cols = lax.broadcasted_iota(jnp.int32, ref.shape, 1)
    far = jnp.abs(rows - cols)
    band = jnp.zeros(ref.shape, jnp.float32)
    for j in range(1, 5):
        band = jnp.where(far == j, split_coeff(coeffs[j])[part], band)
    ref[...] = band.astype(jnp.bfloat16)


def kernel(
    n_gx,
    n_shot,
    code_ref,
    assign_ref,
    px_ref,
    py_ref,
    wav_ref,
    speed_hbm,
    press_hbm,
    prev_hbm,
    traces_hbm,
    out_hbm,
    misfit_hbm,
    field,
    speed,
    traces,
    obs,
    obs_send,
    obs_recv,
    pack,
    pack_recv,
    sources,
    record,
    record_in,
    misfit,
    band_hi,
    band_lo,
    x_send,
    x_recv,
    z_send,
    z_recv,
    load_sem,
    swap_send,
    swap_recv,
    traces_sem,
    pack_send,
    pack_rsem,
    obs_ssem,
    obs_rsem,
    rec_send,
    rec_recv,
    out_sem,
    out_send,
    out_recv,
    mis_sem,
):
    gx = lax.axis_index("gx")
    core = lax.axis_index("gy")
    shot = lax.axis_index("shot")
    depth = speed_hbm.shape[0]
    half = depth // 2
    wide = speed_hbm.shape[1]
    steps = record.shape[1]
    nsh = code_ref.shape[0]
    nchunk = half // CH
    own = pl.ds(ROW, wide)
    has_left = gx > 0
    has_right = gx < n_gx - 1
    other = 1 - core

    def shot_at(d):
        return lax.rem(shot + d, n_shot)

    def x_copy(slot, side, chunk):
        z = pl.ds(4 + CH * chunk, CH)
        if side == 0:
            src, dst, to = pl.ds(ROW, 4), pl.ds(ROW + wide, 4), gx - 1
        else:
            src, dst, to = pl.ds(ROW + wide - 4, 4), pl.ds(ROW - 4, 4), gx + 1
        return pltpu.make_async_remote_copy(
            src_ref=field.at[slot, :, z, src, :],
            dst_ref=field.at[slot, :, z, dst, :],
            send_sem=x_send.at[slot, side, chunk],
            recv_sem=x_recv.at[slot, side, chunk],
            device_id={"gx": to},
            device_id_type=MESH,
        )

    def z_copy(slot):
        src = jnp.where(core == 0, half, 4)
        dst = jnp.where(core == 0, 0, 4 + half)
        return pltpu.make_async_remote_copy(
            src_ref=field.at[slot, :, pl.ds(src, 4), own, :],
            dst_ref=field.at[slot, :, pl.ds(dst, 4), own, :],
            send_sem=z_send.at[slot],
            recv_sem=z_recv.at[slot],
            device_id={"gy": other},
            device_id_type=MESH,
        )

    def start_x(slot, chunk):
        @pl.when(has_left)
        def _():
            x_copy(slot, 0, chunk).start()

        @pl.when(has_right)
        def _():
            x_copy(slot, 1, chunk).start()

    def wait_x_recv(slot, chunk):
        @pl.when(has_right)
        def _():
            x_copy(slot, 0, chunk).wait_recv()

        @pl.when(has_left)
        def _():
            x_copy(slot, 1, chunk).wait_recv()

    def wait_x_send(slot, chunk):
        @pl.when(has_left)
        def _():
            x_copy(slot, 0, chunk).wait_send()

        @pl.when(has_right)
        def _():
            x_copy(slot, 1, chunk).wait_send()

    def place_of(which):
        if which == 0:
            return press_hbm.at[0], field.at[0, core, pl.ds(4, half), own, :]
        if which == 1:
            return speed_hbm, speed.at[core]
        return prev_hbm.at[0], field.at[1, core, pl.ds(4, half), own, :]

    def load(which):
        src, dst = place_of(which)
        return pltpu.make_async_copy(
            src.at[pl.ds(core * half, half)], dst, load_sem.at[which]
        )

    def swap(which):
        src, dst = place_of(which)
        return pltpu.make_async_remote_copy(
            src_ref=src.at[pl.ds(other * half, half)],
            dst_ref=dst,
            send_sem=swap_send.at[which],
            recv_sem=swap_recv.at[which],
            device_id={"gy": other},
            device_id_type=MESH,
        )

    def pack_copy(d):
        return pltpu.make_async_remote_copy(
            src_ref=pack,
            dst_ref=pack_recv.at[d - 1],
            send_sem=pack_send.at[d - 1],
            recv_sem=pack_rsem.at[d - 1],
            device_id={"shot": shot_at(d)},
            device_id_type=MESH,
        )

    def obs_copy(d):
        return pltpu.make_async_remote_copy(
            src_ref=obs_send.at[d - 1],
            dst_ref=obs_recv.at[d - 1],
            send_sem=obs_ssem.at[d - 1],
            recv_sem=obs_rsem.at[d - 1],
            device_id={"shot": shot_at(d)},
            device_id_type=MESH,
        )

    for which in range(3):
        load(which).start()
    traces_in = pltpu.make_async_copy(traces_hbm, traces, traces_sem)
    traces_in.start()

    for slot in range(2):
        for h in range(2):
            rows = field.shape[3]
            field[slot, h, :, 0:ROW, :] = jnp.zeros((half + 8, ROW, 128), jnp.float32)
            field[slot, h, :, ROW + wide :, :] = jnp.zeros(
                (half + 8, rows - ROW - wide, 128), jnp.float32
            )
            field[slot, h, 0:4, own, :] = jnp.zeros((4, wide, 128), jnp.float32)
            field[slot, h, 4 + half :, own, :] = jnp.zeros((4, wide, 128), jnp.float32)

    barrier = pltpu.get_barrier_semaphore()

    @pl.when(has_left)
    def _():
        pl.semaphore_signal(barrier, inc=1, device_id={"gx": gx - 1}, device_id_type=MESH)

    @pl.when(has_right)
    def _():
        pl.semaphore_signal(barrier, inc=1, device_id={"gx": gx + 1}, device_id_type=MESH)

    pl.semaphore_signal(barrier, inc=1, device_id={"gy": other}, device_id_type=MESH)
    for d in range(1, n_shot):
        pl.semaphore_signal(
            barrier, inc=1, device_id={"shot": shot_at(d)}, device_id_type=MESH
        )
    greeted = n_shot + has_left.astype(jnp.int32) + has_right.astype(jnp.int32)
    pl.semaphore_wait(barrier, greeted)

    for which in range(3):
        swap(which).start()

    lane = lax.broadcasted_iota(jnp.int32, (1, 128), 1)
    lane8 = lax.broadcasted_iota(jnp.int32, (nsh, 128), 1)
    sub8 = lax.broadcasted_iota(jnp.int32, (nsh, 128), 0)
    rows3 = [jnp.zeros((1, 128), jnp.int32) for _ in range(3)]
    signed = jnp.zeros((nsh, 128), jnp.float32)
    signs = [(2 * code_ref[s] - 1).astype(jnp.float32) for s in range(nsh)]
    for s in range(nsh):
        mine = lane == shot * nsh + s
        for r, ref in enumerate((assign_ref, px_ref, py_ref)):
            rows3[r] = jnp.where(mine, ref[s], rows3[r])
        signed = jnp.where((lane8 == shot * nsh + s) & (sub8 == s), signs[s], signed)
    pack[0:steps, :] = lax.dot_general(
        wav_ref[...], signed, (((0,), (0,)), ((), ())), precision=HIGHEST,
        preferred_element_type=jnp.float32,
    )
    for r in range(3):
        pack[steps + r : steps + r + 1, :] = rows3[r].astype(jnp.float32)
    pack[steps + 3 :, :] = jnp.zeros((pack.shape[0] - steps - 3, 128), jnp.float32)
    for d in range(1, n_shot):
        pack_copy(d).start()

    fill_band(band_hi, 0)
    fill_band(band_lo, 1)

    def chunk_of(i):
        return jnp.where(core == 0, nchunk - 1 - i, i)

    load(0).wait()
    swap(0).wait_recv()
    z_copy(0).start()
    for i in range(nchunk):
        start_x(0, chunk_of(i))

    traces_in.wait()
    for d in range(1, n_shot):
        target = shot_at(d)
        scale = [jnp.where(assign_ref[s] == target, signs[s], 0.0) for s in range(nsh)]

        def part(t, carry, scale=scale, d=d):
            total = scale[0] * traces[0, t]
            for s in range(1, nsh):
                total += scale[s] * traces[s, t]
            obs_send[d - 1, t] = total
            return carry

        lax.fori_loop(0, steps, part, 0)
        obs_copy(d).start()
    scale_own = [jnp.where(assign_ref[s] == shot, signs[s], 0.0) for s in range(nsh)]

    def part_own(t, carry):
        total = scale_own[0] * traces[0, t]
        for s in range(1, nsh):
            total += scale_own[s] * traces[s, t]
        obs[t] = total
        return carry

    lax.fori_loop(0, steps, part_own, 0)

    table = pack[...]
    for d in range(1, n_shot):
        pack_copy(d).wait_recv()
        table = table + pack_recv[d - 1]
    weight = jnp.where(
        table[steps : steps + 1] == shot.astype(jnp.float32), table[0:steps], 0.0
    )
    weight = weight * jnp.where(core == 0, 1.0, 0.0)
    local_x = table[steps + 1 : steps + 2] - (gx * wide).astype(jnp.float32)
    onex = jnp.where(
        local_x == lax.broadcasted_iota(jnp.int32, (wide, 128), 0).astype(jnp.float32), 1.0, 0.0
    )
    oney = jnp.where(
        table[steps + 2 : steps + 3]
        == lax.broadcasted_iota(jnp.int32, (256, 128), 0).astype(jnp.float32),
        1.0,
        0.0,
    )
    left = (weight[:, None, :] * onex[None]).reshape(steps * wide, 128)
    grid = lax.dot_general(
        left, oney, (((1,), (1,)), ((), ())), precision=HIGHEST,
        preferred_element_type=jnp.float32,
    )
    for h in range(2):
        sources[h] = grid[:, 128 * h : 128 * (h + 1)].reshape(steps, wide, 128)

    for which in range(1, 3):
        load(which).wait()
        swap(which).wait_recv()

    def one_chunk(n, i):
        now = lax.rem(n, 2)
        new = 1 - now
        chunk = chunk_of(i)
        z0 = 4 + CH * chunk
        zs = pl.ds(z0, CH)
        if i == 0:
            z_copy(now).wait_recv()

            @pl.when(n > 0)
            def _():
                z_copy(new).wait_send()

        wait_x_recv(now, chunk)

        @pl.when(n > 0)
        def _():
            wait_x_send(new, chunk)

        center = [field[now, h, zs, own, :] for h in range(2)]
        both = jnp.concatenate([v.reshape(CH * wide, 128) for v in center], axis=1)
        hi = both.astype(jnp.bfloat16)
        lo = (both - hi.astype(jnp.float32)).astype(jnp.bfloat16)
        dot = functools.partial(jnp.dot, preferred_element_type=jnp.float32)
        along_y = dot(hi, band_hi[...]) + dot(lo, band_hi[...]) + dot(hi, band_lo[...])
        for h in range(2):
            total = along_y[:, 128 * h : 128 * (h + 1)].reshape(CH, wide, 128)
            total = total + (3.0 * coeffs[0]) * center[h]
            for j in range(1, 5):
                ring = (
                    field[now, h, pl.ds(z0 + j, CH), own, :]
                    + field[now, h, pl.ds(z0 - j, CH), own, :]
                ) + (
                    field[now, h, zs, pl.ds(ROW + j, wide), :]
                    + field[now, h, zs, pl.ds(ROW - j, wide), :]
                )
                total = total + coeffs[j] * ring
            field[new, h, zs, own, :] = (
                2.0 * center[h] - field[new, h, zs, own, :]
                + speed[h, pl.ds(CH * chunk, CH)] * total
            )

        @pl.when((core == 0) & (chunk == 0))
        def _():
            for h in range(2):
                at = 4 + source_layer
                field[new, h, at, own, :] = field[new, h, at, own, :] + sources[h, n]
                record[h, n] = field[new, h, 4 + record_layer, own, :]

        @pl.when(n < steps - 1)
        def _():
            if i == 0:
                z_copy(new).start()
            start_x(new, chunk)

    def one_step(n, carry):
        for i in range(nchunk):
            one_chunk(n, i)
        return carry

    lax.fori_loop(0, steps, one_step, 0)

    last = steps % 2
    rest = 1 - last
    out_own = pltpu.make_async_copy(
        field.at[last, core, pl.ds(4, half), own, :],
        out_hbm.at[0, pl.ds(core * half, half)],
        out_sem,
    )
    out_own.start()
    out_away = pltpu.make_async_remote_copy(
        src_ref=field.at[last, other, pl.ds(4, half), own, :],
        dst_ref=out_hbm.at[0, pl.ds(core * half, half)],
        send_sem=out_send,
        recv_sem=out_recv,
        device_id={"gy": other},
        device_id_type=MESH,
    )
    out_away.start()
    rec_copy = pltpu.make_async_remote_copy(
        src_ref=record.at[1],
        dst_ref=record_in,
        send_sem=rec_send,
        recv_sem=rec_recv,
        device_id={"gy": other},
        device_id_type=MESH,
    )

    @pl.when(core == 0)
    def _():
        rec_copy.start()

    observed = obs[...]
    for d in range(1, n_shot):
        obs_copy(d).wait_recv()
        observed = observed + obs_recv[d - 1]

    @pl.when(core == 0)
    def _():
        misfit[...] = record[0] - observed

    @pl.when(core == 1)
    def _():
        rec_copy.wait_recv()
        misfit[...] = record_in[...] - observed

    mis = pltpu.make_async_copy(misfit, misfit_hbm.at[0], mis_sem)
    mis.start()

    z_copy(rest).wait_send()
    for i in range(nchunk):
        wait_x_send(rest, i)
    for which in range(3):
        swap(which).wait_send()
    for d in range(1, n_shot):
        pack_copy(d).wait_send()
        obs_copy(d).wait_send()

    @pl.when(core == 0)
    def _():
        rec_copy.wait_send()

    out_own.wait()
    out_away.wait()
    mis.wait()


def on_device(n_gx, n_shot, speed, pressure, previous, wavelets, traces, code, assign, px, py):
    depth, wide, wide_y = speed.shape
    nsh, steps = wavelets.shape
    half = depth // 2
    pairs = max(n_shot - 1, 1)
    f32 = jnp.float32
    smem = pl.BlockSpec(memory_space=pltpu.SMEM)
    any_ = pl.BlockSpec(memory_space=pl.ANY)
    dma = pltpu.SemaphoreType.DMA
    nchunk = half // CH
    return pl.pallas_call(
        functools.partial(kernel, n_gx, n_shot),
        out_shape=(
            jax.ShapeDtypeStruct((1, depth, wide, wide_y), f32),
            jax.ShapeDtypeStruct((1, steps, wide, wide_y), f32),
        ),
        in_specs=[smem] * 4 + [pl.BlockSpec(memory_space=pltpu.VMEM)] + [any_] * 4,
        out_specs=(any_, any_),
        scratch_shapes=[
            pltpu.VMEM((2, 2, half + 8, wide + 16, wide_y), f32),
            pltpu.VMEM((2, half, wide, wide_y), f32),
            pltpu.VMEM((nsh, steps, wide, wide_y), f32),
            pltpu.VMEM((steps, wide, wide_y), f32),
            pltpu.VMEM((pairs, steps, wide, wide_y), f32),
            pltpu.VMEM((pairs, steps, wide, wide_y), f32),
            pltpu.VMEM((-(-(steps + 3) // 8) * 8, 128), f32),
            pltpu.VMEM((pairs, -(-(steps + 3) // 8) * 8, 128), f32),
            pltpu.VMEM((2, steps, wide, wide_y), f32),
            pltpu.VMEM((2, steps, wide, wide_y), f32),
            pltpu.VMEM((steps, wide, wide_y), f32),
            pltpu.VMEM((steps, wide, wide_y), f32),
            pltpu.VMEM((2 * wide_y, 2 * wide_y), jnp.bfloat16),
            pltpu.VMEM((2 * wide_y, 2 * wide_y), jnp.bfloat16),
            dma((2, 2, nchunk)),
            dma((2, 2, nchunk)),
            dma((2,)),
            dma((2,)),
            dma((3,)),
            dma((3,)),
            dma((3,)),
            dma,
            dma((pairs,)),
            dma((pairs,)),
            dma((pairs,)),
            dma((pairs,)),
            dma,
            dma,
            dma,
            dma,
            dma,
            dma,
        ],
        compiler_params=pltpu.CompilerParams(
            collective_id=0, has_side_effects=True, vmem_limit_bytes=40 * 1024 * 1024
        ),
    )(code, assign, px, py, wavelets, speed, pressure, previous, traces)


def solution(mesh):
    return jax.shard_map(
        functools.partial(on_device, mesh.shape["gx"], mesh.shape["shot"]),
        mesh=mesh,
        in_specs=(
            P("grp", "gx", "gy"),
            P(("grp", "shot"), None, "gx", "gy"),
            P(("grp", "shot"), None, "gx", "gy"),
            P(("grp", "shot"), None),
            P(("grp", "shot"), None, "gx", "gy"),
            P(("grp", "shot")),
            P(("grp", "shot")),
            P(("grp", "shot")),
            P(("grp", "shot")),
        ),
        out_specs=(P(("grp", "shot"), None, "gx", "gy"), P(("grp", "shot"), None, "gx", "gy")),
        check_vma=False,
    )
```

```python
import functools

import jax
import jax.numpy as jnp
import ml_dtypes
from jax import lax
from jax.experimental import pallas as pl
from jax.experimental.pallas import tpu as pltpu
from jax.sharding import PartitionSpec as P

coeffs = (-205.0 / 72.0, 8.0 / 5.0, -1.0 / 5.0, 8.0 / 315.0, -1.0 / 560.0)
source_layer = 2
record_layer = 6
MESH = pl.DeviceIdType.MESH
HIGHEST = lax.Precision.HIGHEST
ROW = 8
CH = 4


def split_coeff(value):
    high = float(ml_dtypes.bfloat16(value))
    low = float(ml_dtypes.bfloat16(value - high))
    return high, low


def fill_band(ref, part):
    size = ref.shape[0]
    rows = lax.broadcasted_iota(jnp.int32, ref.shape, 0)
    cols = lax.broadcasted_iota(jnp.int32, ref.shape, 1)
    far = jnp.abs(rows - cols)
    band = jnp.zeros(ref.shape, jnp.float32)
    for j in range(1, 5):
        band = jnp.where(far == j, split_coeff(coeffs[j])[part], band)
    ref[...] = band.astype(jnp.bfloat16)


def kernel(
    n_gx,
    n_shot,
    code_hbm,
    assign_hbm,
    px_hbm,
    py_hbm,
    wav_hbm,
    speed_hbm,
    press_hbm,
    prev_hbm,
    traces_hbm,
    out_hbm,
    misfit_hbm,
    code_ref,
    assign_ref,
    px_ref,
    py_ref,
    wav_ref,
    field,
    speed,
    traces,
    obs,
    obs_send,
    obs_recv,
    pack,
    pack_recv,
    sources,
    record,
    record_in,
    misfit,
    band_hi,
    band_lo,
    x_send,
    x_recv,
    z_send,
    z_recv,
    load_sem,
    swap_send,
    swap_recv,
    traces_sem,
    small_sem,
    init_send,
    pack_send,
    pack_rsem,
    obs_ssem,
    obs_rsem,
    rec_send,
    rec_recv,
    out_sem,
    out_send,
    out_recv,
    mis_sem,
):
    gx = lax.axis_index("gx")
    core = lax.axis_index("gy")
    shot = lax.axis_index("shot")
    depth = speed_hbm.shape[0]
    half = depth // 2
    wide = speed_hbm.shape[1]
    steps = record.shape[1]
    nsh = code_ref.shape[0]
    last = steps % 2
    rest = 1 - last
    nchunk = half // CH
    own = pl.ds(ROW, wide)
    has_left = gx > 0
    has_right = gx < n_gx - 1
    other = 1 - core

    def shot_at(d):
        return lax.rem(shot + d, n_shot)

    def x_copy(slot, side, chunk):
        z = pl.ds(4 + CH * chunk, CH)
        if side == 0:
            src, dst, to = pl.ds(ROW, 4), pl.ds(ROW + wide, 4), gx - 1
        else:
            src, dst, to = pl.ds(ROW + wide - 4, 4), pl.ds(ROW - 4, 4), gx + 1
        return pltpu.make_async_remote_copy(
            src_ref=field.at[slot, :, z, src, :],
            dst_ref=field.at[slot, :, z, dst, :],
            send_sem=x_send.at[slot, side, chunk],
            recv_sem=x_recv.at[slot, side, chunk],
            device_id={"gx": to},
            device_id_type=MESH,
        )

    def z_copy(slot):
        src = jnp.where(core == 0, half, 4)
        dst = jnp.where(core == 0, 0, 4 + half)
        return pltpu.make_async_remote_copy(
            src_ref=field.at[slot, :, pl.ds(src, 4), own, :],
            dst_ref=field.at[slot, :, pl.ds(dst, 4), own, :],
            send_sem=z_send.at[slot],
            recv_sem=z_recv.at[slot],
            device_id={"gy": other},
            device_id_type=MESH,
        )

    def start_x(slot, chunk):
        @pl.when(has_left)
        def _():
            x_copy(slot, 0, chunk).start()

        @pl.when(has_right)
        def _():
            x_copy(slot, 1, chunk).start()

    def wait_x_recv(slot, chunk):
        @pl.when(has_right)
        def _():
            x_copy(slot, 0, chunk).wait_recv()

        @pl.when(has_left)
        def _():
            x_copy(slot, 1, chunk).wait_recv()

    def wait_x_send(slot, chunk):
        @pl.when(has_left)
        def _():
            x_copy(slot, 0, chunk).wait_send()

        @pl.when(has_right)
        def _():
            x_copy(slot, 1, chunk).wait_send()

    def place_of(which, to):
        if which == 0:
            src = press_hbm.at[0, pl.ds(to * (half - 4), half + 4)]
            return src, field.at[0, core, pl.ds(4 * (1 - to), half + 4), own, :]
        if which == 1:
            return speed_hbm.at[pl.ds(to * half, half)], speed.at[core]
        src = prev_hbm.at[0, pl.ds(to * half, half)]
        return src, field.at[1, core, pl.ds(4, half), own, :]

    def load(which):
        src, dst = place_of(which, core)
        return pltpu.make_async_copy(src, dst, load_sem.at[which])

    def swap(which):
        src, dst = place_of(which, other)
        return pltpu.make_async_remote_copy(
            src_ref=src,
            dst_ref=dst,
            send_sem=swap_send.at[which],
            recv_sem=swap_recv.at[which],
            device_id={"gy": other},
            device_id_type=MESH,
        )

    def init_copy(side, to, chunk):
        if side == 0:
            src, dst, nb = pl.ds(0, 4), pl.ds(ROW + wide, 4), gx - 1
        else:
            src, dst, nb = pl.ds(wide - 4, 4), pl.ds(ROW - 4, 4), gx + 1
        index = jnp.where(to == 0, nchunk - 1 - chunk, chunk)
        return pltpu.make_async_remote_copy(
            src_ref=press_hbm.at[0, pl.ds(to * half + CH * index, CH), src, :],
            dst_ref=field.at[0, core, pl.ds(4 + CH * index, CH), dst, :],
            send_sem=init_send.at[side, jnp.where(to == core, 0, 1), chunk],
            recv_sem=x_recv.at[0, side, index],
            device_id={"gx": nb, "gy": to},
            device_id_type=MESH,
        )

    def each_init(act):
        for chunk in range(nchunk):
            for to in (core, other):

                @pl.when(has_left)
                def _(chunk=chunk, to=to):
                    act(init_copy(0, to, chunk))

                @pl.when(has_right)
                def _(chunk=chunk, to=to):
                    act(init_copy(1, to, chunk))

    def out_copy(chunk):
        return pltpu.make_async_copy(
            field.at[last, core, pl.ds(4 + CH * chunk, CH), own, :],
            out_hbm.at[0, pl.ds(core * half + CH * chunk, CH)],
            out_sem.at[chunk],
        )

    def out_away(chunk):
        return pltpu.make_async_remote_copy(
            src_ref=field.at[last, other, pl.ds(4 + CH * chunk, CH), own, :],
            dst_ref=out_hbm.at[0, pl.ds(core * half + CH * chunk, CH)],
            send_sem=out_send.at[chunk],
            recv_sem=out_recv.at[chunk],
            device_id={"gy": other},
            device_id_type=MESH,
        )

    def rec_copy(which):
        rows = pl.ds(0, steps - 1) if which == 0 else pl.ds(steps - 1, 1)
        return pltpu.make_async_remote_copy(
            src_ref=record.at[1, rows],
            dst_ref=record_in.at[rows],
            send_sem=rec_send.at[which],
            recv_sem=rec_recv.at[which],
            device_id={"gy": other},
            device_id_type=MESH,
        )

    def pack_copy(d):
        return pltpu.make_async_remote_copy(
            src_ref=pack,
            dst_ref=pack_recv.at[d - 1],
            send_sem=pack_send.at[d - 1],
            recv_sem=pack_rsem.at[d - 1],
            device_id={"shot": shot_at(d)},
            device_id_type=MESH,
        )

    def obs_copy(d):
        return pltpu.make_async_remote_copy(
            src_ref=obs_send.at[d - 1],
            dst_ref=obs_recv.at[d - 1],
            send_sem=obs_ssem.at[d - 1],
            recv_sem=obs_rsem.at[d - 1],
            device_id={"shot": shot_at(d)},
            device_id_type=MESH,
        )

    barrier = pltpu.get_barrier_semaphore()

    def greet(device):
        pl.semaphore_signal(barrier, inc=1, device_id=device, device_id_type=MESH)

    @pl.when(has_left)
    def _():
        for to in (core, other):
            greet({"gx": gx - 1, "gy": to})

    @pl.when(has_right)
    def _():
        for to in (core, other):
            greet({"gx": gx + 1, "gy": to})

    greet({"gy": other})
    for d in range(1, n_shot):
        greet({"shot": shot_at(d)})

    small = [
        pltpu.make_async_copy(src, dst, small_sem.at[i])
        for i, (src, dst) in enumerate(
            (
                (code_hbm, code_ref),
                (assign_hbm, assign_ref),
                (px_hbm, px_ref),
                (py_hbm, py_ref),
                (wav_hbm, wav_ref),
            )
        )
    ]
    for copy in small:
        copy.start()
    for which in range(3):
        load(which).start()
    traces_in = pltpu.make_async_copy(traces_hbm, traces, traces_sem)
    traces_in.start()

    greeted = n_shot + 2 * (has_left.astype(jnp.int32) + has_right.astype(jnp.int32))
    pl.semaphore_wait(barrier, greeted)
    swap(0).start()
    each_init(lambda copy: copy.start())
    for which in (1, 2):
        swap(which).start()

    for slot in range(2):
        for h in range(2):

            @pl.when(jnp.logical_not(has_left))
            def _(slot=slot, h=h):
                field[slot, h, :, 0:ROW, :] = jnp.zeros((half + 8, ROW, 128), jnp.float32)

            @pl.when(jnp.logical_not(has_right))
            def _(slot=slot, h=h):
                field[slot, h, :, ROW + wide :, :] = jnp.zeros((half + 8, 8, 128), jnp.float32)

            field[slot, h, pl.ds(core * (half + 4), 4), own, :] = jnp.zeros(
                (4, wide, 128), jnp.float32
            )

    for copy in small:
        copy.wait()

    lane = lax.broadcasted_iota(jnp.int32, (1, 128), 1)
    lane8 = lax.broadcasted_iota(jnp.int32, (nsh, 128), 1)
    sub8 = lax.broadcasted_iota(jnp.int32, (nsh, 128), 0)
    rows3 = [jnp.zeros((1, 128), jnp.int32) for _ in range(3)]
    signed = jnp.zeros((nsh, 128), jnp.float32)
    signs = [(2 * code_ref[s] - 1).astype(jnp.float32) for s in range(nsh)]
    for s in range(nsh):
        mine = lane == shot * nsh + s
        for r, ref in enumerate((assign_ref, px_ref, py_ref)):
            rows3[r] = jnp.where(mine, ref[s], rows3[r])
        signed = jnp.where((lane8 == shot * nsh + s) & (sub8 == s), signs[s], signed)
    pack[0:steps, :] = lax.dot_general(
        wav_ref[...], signed, (((0,), (0,)), ((), ())), precision=HIGHEST,
        preferred_element_type=jnp.float32,
    )
    for r in range(3):
        pack[steps + r : steps + r + 1, :] = rows3[r].astype(jnp.float32)
    pack[steps + 3 :, :] = jnp.zeros((pack.shape[0] - steps - 3, 128), jnp.float32)
    for d in range(1, n_shot):
        pack_copy(d).start()

    fill_band(band_hi, 0)
    fill_band(band_lo, 1)

    def chunk_of(i):
        return jnp.where(core == 0, nchunk - 1 - i, i)

    owners = [shot_at(d) for d in range(n_shot)]
    scales = [
        [jnp.where(assign_ref[k] == owner, signs[k], 0.0) for k in range(nsh)]
        for owner in owners
    ]

    def encode_rows(first, count):
        for r in range(count):
            t = first + r
            rows = [traces[k, t] for k in range(nsh)]
            for d in range(n_shot):
                total = scales[d][0] * rows[0]
                for k in range(1, nsh):
                    total += scales[d][k] * rows[k]
                if d == 0:
                    obs[t] = total
                else:
                    obs_send[d - 1, t] = total

    table = pack[...]
    for d in range(1, n_shot):
        pack_copy(d).wait_recv()
        table = table + pack_recv[d - 1]
    weight = jnp.where(
        table[steps : steps + 1] == shot.astype(jnp.float32), table[0:steps], 0.0
    )
    weight = weight * jnp.where(core == 0, 1.0, 0.0)
    local_x = table[steps + 1 : steps + 2] - (gx * wide).astype(jnp.float32)
    onex = jnp.where(
        local_x == lax.broadcasted_iota(jnp.int32, (wide, 128), 0).astype(jnp.float32), 1.0, 0.0
    )
    oney = jnp.where(
        table[steps + 2 : steps + 3]
        == lax.broadcasted_iota(jnp.int32, (256, 128), 0).astype(jnp.float32),
        1.0,
        0.0,
    )
    left = (weight[:, None, :] * onex[None]).reshape(steps * wide, 128)
    grid = lax.dot_general(
        left, oney, (((1,), (1,)), ((), ())), precision=HIGHEST,
        preferred_element_type=jnp.float32,
    )
    for h in range(2):
        sources[h] = grid[:, 128 * h : 128 * (h + 1)].reshape(steps, wide, 128)

    for which in range(3):
        load(which).wait()
        swap(which).wait_recv()
    traces_in.wait()

    def one_chunk(n, i):
        now = lax.rem(n, 2)
        new = 1 - now
        chunk = chunk_of(i)
        z0 = 4 + CH * chunk
        zs = pl.ds(z0, CH)
        if i == 0:

            @pl.when(n > 0)
            def _():
                z_copy(now).wait_recv()

            @pl.when(n > 1)
            def _():
                z_copy(new).wait_send()

        wait_x_recv(now, chunk)

        @pl.when(n > 1)
        def _():
            wait_x_send(new, chunk)

        center = [field[now, h, zs, own, :] for h in range(2)]
        both = jnp.concatenate([v.reshape(CH * wide, 128) for v in center], axis=1)
        hi = both.astype(jnp.bfloat16)
        lo = (both - hi.astype(jnp.float32)).astype(jnp.bfloat16)
        dot = functools.partial(jnp.dot, preferred_element_type=jnp.float32)
        along_y = dot(hi, band_hi[...]) + dot(lo, band_hi[...]) + dot(hi, band_lo[...])
        for h in range(2):
            total = along_y[:, 128 * h : 128 * (h + 1)].reshape(CH, wide, 128)
            total = total + (3.0 * coeffs[0]) * center[h]
            for j in range(1, 5):
                ring = (
                    field[now, h, pl.ds(z0 + j, CH), own, :]
                    + field[now, h, pl.ds(z0 - j, CH), own, :]
                ) + (
                    field[now, h, zs, pl.ds(ROW + j, wide), :]
                    + field[now, h, zs, pl.ds(ROW - j, wide), :]
                )
                total = total + coeffs[j] * ring
            field[new, h, zs, own, :] = (
                2.0 * center[h] - field[new, h, zs, own, :]
                + speed[h, pl.ds(CH * chunk, CH)] * total
            )

        @pl.when((core == 0) & (chunk == 0))
        def _():
            for h in range(2):
                at = 4 + source_layer
                field[new, h, at, own, :] = field[new, h, at, own, :] + sources[h, n]
                record[h, n] = field[new, h, 4 + record_layer, own, :]

        @pl.when(n < steps - 1)
        def _():
            if i == 0:
                z_copy(new).start()
            start_x(new, chunk)

        @pl.when(n == steps - 1)
        def _():
            out_away(chunk).start()
            out_copy(chunk).start()

    batch = 2
    encoding = -(-steps // batch)

    def one_step(n, carry):
        for i in range(nchunk):
            one_chunk(n, i)

        @pl.when(n < encoding)
        def _():
            encode_rows(n * batch, batch)

        @pl.when(n == encoding)
        def _():
            for d in range(1, n_shot):
                obs_copy(d).start()

        @pl.when((n == steps - 2) & (core == 0))
        def _():
            rec_copy(0).start()

        return carry

    lax.fori_loop(0, steps, one_step, 0)

    @pl.when(core == 0)
    def _():
        rec_copy(1).start()

    observed = obs[...]
    for d in range(1, n_shot):
        obs_copy(d).wait_recv()
        observed = observed + obs_recv[d - 1]

    @pl.when(core == 0)
    def _():
        misfit[...] = record[0] - observed

    @pl.when(core == 1)
    def _():
        rec_copy(0).wait_recv()
        rec_copy(1).wait_recv()
        misfit[...] = record_in[...] - observed

    mis = pltpu.make_async_copy(misfit, misfit_hbm.at[0], mis_sem)
    mis.start()

    z_copy(rest).wait_send()
    for i in range(nchunk):
        wait_x_send(rest, i)
    for which in range(3):
        swap(which).wait_send()
    for d in range(1, n_shot):
        pack_copy(d).wait_send()
        obs_copy(d).wait_send()

    @pl.when(core == 0)
    def _():
        rec_copy(0).wait_send()
        rec_copy(1).wait_send()

    each_init(lambda copy: copy.wait_send())
    for chunk in range(nchunk):
        out_copy(chunk).wait()
        out_away(chunk).wait()
    mis.wait()


def on_device(n_gx, n_shot, speed, pressure, previous, wavelets, traces, code, assign, px, py):
    depth, wide, wide_y = speed.shape
    nsh, steps = wavelets.shape
    half = depth // 2
    pairs = max(n_shot - 1, 1)
    f32 = jnp.float32
    hbm = pl.BlockSpec(memory_space=pltpu.HBM)
    dma = pltpu.SemaphoreType.DMA
    nchunk = half // CH
    return pl.pallas_call(
        functools.partial(kernel, n_gx, n_shot),
        out_shape=(
            jax.ShapeDtypeStruct((1, depth, wide, wide_y), f32),
            jax.ShapeDtypeStruct((1, steps, wide, wide_y), f32),
        ),
        in_specs=[hbm] * 9,
        out_specs=(hbm, hbm),
        scratch_shapes=[
            pltpu.SMEM((nsh,), jnp.int32),
            pltpu.SMEM((nsh,), jnp.int32),
            pltpu.SMEM((nsh,), jnp.int32),
            pltpu.SMEM((nsh,), jnp.int32),
            pltpu.VMEM((nsh, steps), f32),
            pltpu.VMEM((2, 2, half + 8, wide + 16, wide_y), f32),
            pltpu.VMEM((2, half, wide, wide_y), f32),
            pltpu.VMEM((nsh, steps, wide, wide_y), f32),
            pltpu.VMEM((steps, wide, wide_y), f32),
            pltpu.VMEM((pairs, steps, wide, wide_y), f32),
            pltpu.VMEM((pairs, steps, wide, wide_y), f32),
            pltpu.VMEM((-(-(steps + 3) // 8) * 8, 128), f32),
            pltpu.VMEM((pairs, -(-(steps + 3) // 8) * 8, 128), f32),
            pltpu.VMEM((2, steps, wide, wide_y), f32),
            pltpu.VMEM((2, steps, wide, wide_y), f32),
            pltpu.VMEM((steps, wide, wide_y), f32),
            pltpu.VMEM((steps, wide, wide_y), f32),
            pltpu.VMEM((2 * wide_y, 2 * wide_y), jnp.bfloat16),
            pltpu.VMEM((2 * wide_y, 2 * wide_y), jnp.bfloat16),
            dma((2, 2, nchunk)),
            dma((2, 2, nchunk)),
            dma((2,)),
            dma((2,)),
            dma((3,)),
            dma((3,)),
            dma((3,)),
            dma,
            dma((5,)),
            dma((2, 2, nchunk)),
            dma((pairs,)),
            dma((pairs,)),
            dma((pairs,)),
            dma((pairs,)),
            dma((2,)),
            dma((2,)),
            dma((nchunk,)),
            dma((nchunk,)),
            dma((nchunk,)),
            dma,
        ],
        compiler_params=pltpu.CompilerParams(
            collective_id=0, has_side_effects=True, vmem_limit_bytes=62 * 1024 * 1024
        ),
    )(code, assign, px, py, wavelets, speed, pressure, previous, traces)


def solution(mesh):
    return jax.shard_map(
        functools.partial(on_device, mesh.shape["gx"], mesh.shape["shot"]),
        mesh=mesh,
        in_specs=(
            P("grp", "gx", "gy"),
            P(("grp", "shot"), None, "gx", "gy"),
            P(("grp", "shot"), None, "gx", "gy"),
            P(("grp", "shot"), None),
            P(("grp", "shot"), None, "gx", "gy"),
            P(("grp", "shot")),
            P(("grp", "shot")),
            P(("grp", "shot")),
            P(("grp", "shot")),
        ),
        out_specs=(P(("grp", "shot"), None, "gx", "gy"), P(("grp", "shot"), None, "gx", "gy")),
        check_vma=False,
    )
```

```python
import functools

import jax
import jax.numpy as jnp
import ml_dtypes
from jax import lax
from jax.experimental import pallas as pl
from jax.experimental.pallas import tpu as pltpu
from jax.sharding import PartitionSpec as P

coeffs = (-205.0 / 72.0, 8.0 / 5.0, -1.0 / 5.0, 8.0 / 315.0, -1.0 / 560.0)
source_layer = 2
record_layer = 6
MESH = pl.DeviceIdType.MESH
HIGHEST = lax.Precision.HIGHEST
ROW = 8
CH = 4


def split_coeff(value):
    high = float(ml_dtypes.bfloat16(value))
    low = float(ml_dtypes.bfloat16(value - high))
    return high, low


def fill_band(ref, part):
    size = ref.shape[0]
    rows = lax.broadcasted_iota(jnp.int32, ref.shape, 0)
    cols = lax.broadcasted_iota(jnp.int32, ref.shape, 1)
    far = jnp.abs(rows - cols)
    band = jnp.zeros(ref.shape, jnp.float32)
    for j in range(1, 5):
        band = jnp.where(far == j, split_coeff(coeffs[j])[part], band)
    ref[...] = band.astype(jnp.bfloat16)


def kernel(
    n_gx,
    n_shot,
    code_hbm,
    assign_hbm,
    px_hbm,
    py_hbm,
    wav_hbm,
    speed_hbm,
    press_hbm,
    prev_hbm,
    traces_hbm,
    out_hbm,
    misfit_hbm,
    code_ref,
    assign_ref,
    px_ref,
    py_ref,
    wav_ref,
    field,
    speed,
    traces,
    obs,
    obs_send,
    obs_recv,
    pack,
    pack_recv,
    sources,
    record,
    record_in,
    misfit,
    band_hi,
    band_lo,
    x_send,
    x_recv,
    z_send,
    z_recv,
    load_sem,
    swap_send,
    swap_recv,
    traces_sem,
    small_sem,
    init_send,
    pack_send,
    pack_rsem,
    obs_ssem,
    obs_rsem,
    rec_send,
    rec_recv,
    out_sem,
    out_send,
    out_recv,
    mis_sem,
):
    gx = lax.axis_index("gx")
    core = lax.axis_index("gy")
    shot = lax.axis_index("shot")
    depth = speed_hbm.shape[0]
    half = depth // 2
    wide = speed_hbm.shape[1]
    steps = record.shape[1]
    nsh = code_ref.shape[0]
    last = steps % 2
    rest = 1 - last
    nchunk = half // CH
    own = pl.ds(ROW, wide)
    has_left = gx > 0
    has_right = gx < n_gx - 1
    other = 1 - core

    def shot_at(d):
        return lax.rem(shot + d, n_shot)

    def x_copy(slot, side, chunk):
        z = pl.ds(4 + CH * chunk, CH)
        if side == 0:
            src, dst, to = pl.ds(ROW, 4), pl.ds(ROW + wide, 4), gx - 1
        else:
            src, dst, to = pl.ds(ROW + wide - 4, 4), pl.ds(ROW - 4, 4), gx + 1
        return pltpu.make_async_remote_copy(
            src_ref=field.at[slot, :, z, src, :],
            dst_ref=field.at[slot, :, z, dst, :],
            send_sem=x_send.at[slot, side, chunk],
            recv_sem=x_recv.at[slot, side, chunk],
            device_id={"gx": to},
            device_id_type=MESH,
        )

    def z_copy(slot):
        src = jnp.where(core == 0, half, 4)
        dst = jnp.where(core == 0, 0, 4 + half)
        return pltpu.make_async_remote_copy(
            src_ref=field.at[slot, :, pl.ds(src, 4), own, :],
            dst_ref=field.at[slot, :, pl.ds(dst, 4), own, :],
            send_sem=z_send.at[slot],
            recv_sem=z_recv.at[slot],
            device_id={"gy": other},
            device_id_type=MESH,
        )

    def start_x(slot, chunk):
        @pl.when(has_left)
        def _():
            x_copy(slot, 0, chunk).start()

        @pl.when(has_right)
        def _():
            x_copy(slot, 1, chunk).start()

    def wait_x_recv(slot, chunk):
        @pl.when(has_right)
        def _():
            x_copy(slot, 0, chunk).wait_recv()

        @pl.when(has_left)
        def _():
            x_copy(slot, 1, chunk).wait_recv()

    def wait_x_send(slot, chunk):
        @pl.when(has_left)
        def _():
            x_copy(slot, 0, chunk).wait_send()

        @pl.when(has_right)
        def _():
            x_copy(slot, 1, chunk).wait_send()

    def place_of(which, to):
        if which == 0:
            src = press_hbm.at[0, pl.ds(to * (half - 4), half + 4)]
            return src, field.at[0, core, pl.ds(4 * (1 - to), half + 4), own, :]
        if which == 1:
            return speed_hbm.at[pl.ds(to * half, half)], speed.at[core]
        src = prev_hbm.at[0, pl.ds(to * half, half)]
        return src, field.at[1, core, pl.ds(4, half), own, :]

    def load(which):
        src, dst = place_of(which, core)
        return pltpu.make_async_copy(src, dst, load_sem.at[which])

    def swap(which):
        src, dst = place_of(which, other)
        return pltpu.make_async_remote_copy(
            src_ref=src,
            dst_ref=dst,
            send_sem=swap_send.at[which],
            recv_sem=swap_recv.at[which],
            device_id={"gy": other},
            device_id_type=MESH,
        )

    def init_copy(side, to, chunk):
        if side == 0:
            src, dst, nb = pl.ds(0, 4), pl.ds(ROW + wide, 4), gx - 1
        else:
            src, dst, nb = pl.ds(wide - 4, 4), pl.ds(ROW - 4, 4), gx + 1
        index = jnp.where(to == 0, nchunk - 1 - chunk, chunk)
        return pltpu.make_async_remote_copy(
            src_ref=press_hbm.at[0, pl.ds(to * half + CH * index, CH), src, :],
            dst_ref=field.at[0, core, pl.ds(4 + CH * index, CH), dst, :],
            send_sem=init_send.at[side, jnp.where(to == core, 0, 1), chunk],
            recv_sem=x_recv.at[0, side, index],
            device_id={"gx": nb, "gy": to},
            device_id_type=MESH,
        )

    def each_init(act):
        for chunk in range(nchunk):
            for to in (core, other):

                @pl.when(has_left)
                def _(chunk=chunk, to=to):
                    act(init_copy(0, to, chunk))

                @pl.when(has_right)
                def _(chunk=chunk, to=to):
                    act(init_copy(1, to, chunk))

    def out_copy(chunk):
        return pltpu.make_async_copy(
            field.at[last, core, pl.ds(4 + CH * chunk, CH), own, :],
            out_hbm.at[0, pl.ds(core * half + CH * chunk, CH)],
            out_sem.at[chunk],
        )

    def out_away(chunk):
        return pltpu.make_async_remote_copy(
            src_ref=field.at[last, other, pl.ds(4 + CH * chunk, CH), own, :],
            dst_ref=out_hbm.at[0, pl.ds(core * half + CH * chunk, CH)],
            send_sem=out_send.at[chunk],
            recv_sem=out_recv.at[chunk],
            device_id={"gy": other},
            device_id_type=MESH,
        )

    def rec_copy(which):
        rows = pl.ds(0, steps - 1) if which == 0 else pl.ds(steps - 1, 1)
        return pltpu.make_async_remote_copy(
            src_ref=record.at[1, rows],
            dst_ref=record_in.at[rows],
            send_sem=rec_send.at[which],
            recv_sem=rec_recv.at[which],
            device_id={"gy": other},
            device_id_type=MESH,
        )

    def pack_copy(d):
        return pltpu.make_async_remote_copy(
            src_ref=pack,
            dst_ref=pack_recv.at[d - 1],
            send_sem=pack_send.at[d - 1],
            recv_sem=pack_rsem.at[d - 1],
            device_id={"shot": shot_at(d)},
            device_id_type=MESH,
        )

    def obs_copy(d):
        return pltpu.make_async_remote_copy(
            src_ref=obs_send.at[d - 1],
            dst_ref=obs_recv.at[d - 1],
            send_sem=obs_ssem.at[d - 1],
            recv_sem=obs_rsem.at[d - 1],
            device_id={"shot": shot_at(d)},
            device_id_type=MESH,
        )

    barrier = pltpu.get_barrier_semaphore()

    def greet(device):
        pl.semaphore_signal(barrier, inc=1, device_id=device, device_id_type=MESH)

    @pl.when(has_left)
    def _():
        for to in (core, other):
            greet({"gx": gx - 1, "gy": to})

    @pl.when(has_right)
    def _():
        for to in (core, other):
            greet({"gx": gx + 1, "gy": to})

    greet({"gy": other})
    for d in range(1, n_shot):
        greet({"shot": shot_at(d)})

    small = [
        pltpu.make_async_copy(src, dst, small_sem.at[i])
        for i, (src, dst) in enumerate(
            (
                (code_hbm, code_ref),
                (assign_hbm, assign_ref),
                (px_hbm, px_ref),
                (py_hbm, py_ref),
                (wav_hbm, wav_ref),
            )
        )
    ]
    for copy in small:
        copy.start()
    for which in range(3):
        load(which).start()
    traces_in = pltpu.make_async_copy(traces_hbm, traces, traces_sem)
    traces_in.start()

    greeted = n_shot + 2 * (has_left.astype(jnp.int32) + has_right.astype(jnp.int32))
    pl.semaphore_wait(barrier, greeted)
    swap(0).start()
    each_init(lambda copy: copy.start())
    for which in (1, 2):
        swap(which).start()

    for slot in range(2):
        for h in range(2):

            @pl.when(jnp.logical_not(has_left))
            def _(slot=slot, h=h):
                field[slot, h, :, 0:ROW, :] = jnp.zeros((half + 8, ROW, 128), jnp.float32)

            @pl.when(jnp.logical_not(has_right))
            def _(slot=slot, h=h):
                field[slot, h, :, ROW + wide :, :] = jnp.zeros((half + 8, 8, 128), jnp.float32)

            field[slot, h, pl.ds(core * (half + 4), 4), own, :] = jnp.zeros(
                (4, wide, 128), jnp.float32
            )

    for copy in small:
        copy.wait()

    lane = lax.broadcasted_iota(jnp.int32, (1, 128), 1)
    lane8 = lax.broadcasted_iota(jnp.int32, (nsh, 128), 1)
    sub8 = lax.broadcasted_iota(jnp.int32, (nsh, 128), 0)
    rows3 = [jnp.zeros((1, 128), jnp.int32) for _ in range(3)]
    signed = jnp.zeros((nsh, 128), jnp.float32)
    signs = [(2 * code_ref[s] - 1).astype(jnp.float32) for s in range(nsh)]
    for s in range(nsh):
        mine = lane == shot * nsh + s
        for r, ref in enumerate((assign_ref, px_ref, py_ref)):
            rows3[r] = jnp.where(mine, ref[s], rows3[r])
        signed = jnp.where((lane8 == shot * nsh + s) & (sub8 == s), signs[s], signed)
    pack[0:steps, :] = lax.dot_general(
        wav_ref[...], signed, (((0,), (0,)), ((), ())), precision=HIGHEST,
        preferred_element_type=jnp.float32,
    )
    for r in range(3):
        pack[steps + r : steps + r + 1, :] = rows3[r].astype(jnp.float32)
    pack[steps + 3 :, :] = jnp.zeros((pack.shape[0] - steps - 3, 128), jnp.float32)
    for d in range(1, n_shot):
        pack_copy(d).start()

    fill_band(band_hi, 0)
    fill_band(band_lo, 1)

    def chunk_of(i):
        return jnp.where(core == 0, nchunk - 1 - i, i)

    owners = [shot_at(d) for d in range(n_shot)]
    scales = [
        [jnp.where(assign_ref[k] == owner, signs[k], 0.0) for k in range(nsh)]
        for owner in owners
    ]

    def encode_rows(first, count):
        for r in range(count):
            t = first + r
            rows = [traces[k, t] for k in range(nsh)]
            for d in range(n_shot):
                total = scales[d][0] * rows[0]
                for k in range(1, nsh):
                    total += scales[d][k] * rows[k]
                if d == 0:
                    obs[t] = total
                else:
                    obs_send[d - 1, t] = total

    for which in range(3):
        load(which).wait()
        swap(which).wait_recv()
    traces_in.wait()

    def make_sources():
        table = pack[...]
        for d in range(1, n_shot):
            table = table + pack_recv[d - 1]
        weight = jnp.where(
            table[steps : steps + 1] == shot.astype(jnp.float32), table[0:steps], 0.0
        )
        local_x = table[steps + 1 : steps + 2] - (gx * wide).astype(jnp.float32)
        onex = jnp.where(
            local_x == lax.broadcasted_iota(jnp.int32, (wide, 128), 0).astype(jnp.float32), 1.0, 0.0
        )
        oney = jnp.where(
            table[steps + 2 : steps + 3]
            == lax.broadcasted_iota(jnp.int32, (256, 128), 0).astype(jnp.float32),
            1.0,
            0.0,
        )
        left = (weight[:, None, :] * onex[None]).reshape(steps * wide, 128)
        grid = lax.dot_general(
            left, oney, (((1,), (1,)), ((), ())), precision=HIGHEST,
            preferred_element_type=jnp.float32,
        )
        for h in range(2):
            sources[h] = grid[:, 128 * h : 128 * (h + 1)].reshape(steps, wide, 128)

    def one_chunk(n, i):
        now = lax.rem(n, 2)
        new = 1 - now
        chunk = chunk_of(i)
        z0 = 4 + CH * chunk
        zs = pl.ds(z0, CH)
        if i == 0:

            @pl.when(n > 0)
            def _():
                z_copy(now).wait_recv()

            @pl.when(n > 1)
            def _():
                z_copy(new).wait_send()

        center = [field[now, h, zs, own, :] for h in range(2)]
        both = jnp.concatenate([v.reshape(CH * wide, 128) for v in center], axis=1)
        hi = both.astype(jnp.bfloat16)
        lo = (both - hi.astype(jnp.float32)).astype(jnp.bfloat16)
        dot = functools.partial(jnp.dot, preferred_element_type=jnp.float32)
        along_y = dot(hi, band_hi[...]) + dot(lo, band_hi[...]) + dot(hi, band_lo[...])
        totals = []
        for h in range(2):
            total = along_y[:, 128 * h : 128 * (h + 1)].reshape(CH, wide, 128)
            total = total + (3.0 * coeffs[0]) * center[h]
            for j in range(1, 5):
                total = total + coeffs[j] * (
                    field[now, h, pl.ds(z0 + j, CH), own, :]
                    + field[now, h, pl.ds(z0 - j, CH), own, :]
                )
            totals.append(total)

        if i == nchunk - 1:

            @pl.when(n == 0)
            def _():
                for d in range(1, n_shot):
                    pack_copy(d).wait_recv()

                @pl.when(core == 0)
                def _():
                    make_sources()

        @pl.when(n > 1)
        def _():
            wait_x_send(new, chunk)

        wait_x_recv(now, chunk)

        for h in range(2):
            total = totals[h]
            for j in range(1, 5):
                total = total + coeffs[j] * (
                    field[now, h, zs, pl.ds(ROW + j, wide), :]
                    + field[now, h, zs, pl.ds(ROW - j, wide), :]
                )
            field[new, h, zs, own, :] = (
                2.0 * field[now, h, zs, own, :] - field[new, h, zs, own, :]
                + speed[h, pl.ds(CH * chunk, CH)] * total
            )

        @pl.when((core == 0) & (chunk == 0))
        def _():
            for h in range(2):
                at = 4 + source_layer
                field[new, h, at, own, :] = field[new, h, at, own, :] + sources[h, n]
                record[h, n] = field[new, h, 4 + record_layer, own, :]

        @pl.when(n < steps - 1)
        def _():
            if i == 0:
                z_copy(new).start()
            start_x(new, chunk)

        @pl.when(n == steps - 1)
        def _():
            out_away(chunk).start()
            out_copy(chunk).start()

    batch = 2
    encoding = -(-steps // batch)

    def one_step(n, carry):
        for i in range(nchunk):
            one_chunk(n, i)

        @pl.when(n < encoding)
        def _():
            encode_rows(n * batch, batch)

        @pl.when(n == encoding)
        def _():
            for d in range(1, n_shot):
                obs_copy(d).start()

        @pl.when((n == steps - 2) & (core == 0))
        def _():
            rec_copy(0).start()

        return carry

    lax.fori_loop(0, steps, one_step, 0)

    @pl.when(core == 0)
    def _():
        rec_copy(1).start()

    def mis_copy(which):
        rows = pl.ds(0, steps - 1) if which == 0 else pl.ds(steps - 1, 1)
        return pltpu.make_async_copy(
            misfit.at[rows], misfit_hbm.at[0, rows], mis_sem.at[which]
        )

    for d in range(1, n_shot):
        obs_copy(d).wait_recv()
    for which in range(2):
        rows = pl.ds(0, steps - 1) if which == 0 else pl.ds(steps - 1, 1)
        observed = obs[rows]
        for d in range(1, n_shot):
            observed = observed + obs_recv[d - 1, rows]

        @pl.when(core == 0)
        def _(rows=rows, observed=observed):
            misfit[rows] = record[0, rows] - observed

        @pl.when(core == 1)
        def _(which=which, rows=rows, observed=observed):
            rec_copy(which).wait_recv()
            misfit[rows] = record_in[rows] - observed

        mis_copy(which).start()

    z_copy(rest).wait_send()
    for i in range(nchunk):
        wait_x_send(rest, i)
    for which in range(3):
        swap(which).wait_send()
    for d in range(1, n_shot):
        pack_copy(d).wait_send()
        obs_copy(d).wait_send()

    @pl.when(core == 0)
    def _():
        rec_copy(0).wait_send()
        rec_copy(1).wait_send()

    each_init(lambda copy: copy.wait_send())
    for chunk in range(nchunk):
        out_copy(chunk).wait()
        out_away(chunk).wait()
    for which in range(2):
        mis_copy(which).wait()


def on_device(n_gx, n_shot, speed, pressure, previous, wavelets, traces, code, assign, px, py):
    depth, wide, wide_y = speed.shape
    nsh, steps = wavelets.shape
    half = depth // 2
    pairs = max(n_shot - 1, 1)
    f32 = jnp.float32
    hbm = pl.BlockSpec(memory_space=pltpu.HBM)
    dma = pltpu.SemaphoreType.DMA
    nchunk = half // CH
    return pl.pallas_call(
        functools.partial(kernel, n_gx, n_shot),
        out_shape=(
            jax.ShapeDtypeStruct((1, depth, wide, wide_y), f32),
            jax.ShapeDtypeStruct((1, steps, wide, wide_y), f32),
        ),
        in_specs=[hbm] * 9,
        out_specs=(hbm, hbm),
        scratch_shapes=[
            pltpu.SMEM((nsh,), jnp.int32),
            pltpu.SMEM((nsh,), jnp.int32),
            pltpu.SMEM((nsh,), jnp.int32),
            pltpu.SMEM((nsh,), jnp.int32),
            pltpu.VMEM((nsh, steps), f32),
            pltpu.VMEM((2, 2, half + 8, wide + 16, wide_y), f32),
            pltpu.VMEM((2, half, wide, wide_y), f32),
            pltpu.VMEM((nsh, steps, wide, wide_y), f32),
            pltpu.VMEM((steps, wide, wide_y), f32),
            pltpu.VMEM((pairs, steps, wide, wide_y), f32),
            pltpu.VMEM((pairs, steps, wide, wide_y), f32),
            pltpu.VMEM((-(-(steps + 3) // 8) * 8, 128), f32),
            pltpu.VMEM((pairs, -(-(steps + 3) // 8) * 8, 128), f32),
            pltpu.VMEM((2, steps, wide, wide_y), f32),
            pltpu.VMEM((2, steps, wide, wide_y), f32),
            pltpu.VMEM((steps, wide, wide_y), f32),
            pltpu.VMEM((steps, wide, wide_y), f32),
            pltpu.VMEM((2 * wide_y, 2 * wide_y), jnp.bfloat16),
            pltpu.VMEM((2 * wide_y, 2 * wide_y), jnp.bfloat16),
            dma((2, 2, nchunk)),
            dma((2, 2, nchunk)),
            dma((2,)),
            dma((2,)),
            dma((3,)),
            dma((3,)),
            dma((3,)),
            dma,
            dma((5,)),
            dma((2, 2, nchunk)),
            dma((pairs,)),
            dma((pairs,)),
            dma((pairs,)),
            dma((pairs,)),
            dma((2,)),
            dma((2,)),
            dma((nchunk,)),
            dma((nchunk,)),
            dma((nchunk,)),
            dma((2,)),
        ],
        compiler_params=pltpu.CompilerParams(
            collective_id=0, has_side_effects=True, vmem_limit_bytes=62 * 1024 * 1024
        ),
    )(code, assign, px, py, wavelets, speed, pressure, previous, traces)


def solution(mesh):
    return jax.shard_map(
        functools.partial(on_device, mesh.shape["gx"], mesh.shape["shot"]),
        mesh=mesh,
        in_specs=(
            P("grp", "gx", "gy"),
            P(("grp", "shot"), None, "gx", "gy"),
            P(("grp", "shot"), None, "gx", "gy"),
            P(("grp", "shot"), None),
            P(("grp", "shot"), None, "gx", "gy"),
            P(("grp", "shot")),
            P(("grp", "shot")),
            P(("grp", "shot")),
            P(("grp", "shot")),
        ),
        out_specs=(P(("grp", "shot"), None, "gx", "gy"), P(("grp", "shot"), None, "gx", "gy")),
        check_vma=False,
    )
```

```python
import functools

import jax
import jax.numpy as jnp
import ml_dtypes
from jax import lax
from jax.experimental import pallas as pl
from jax.experimental.pallas import tpu as pltpu
from jax.sharding import PartitionSpec as P

coeffs = (-205.0 / 72.0, 8.0 / 5.0, -1.0 / 5.0, 8.0 / 315.0, -1.0 / 560.0)
source_layer = 2
record_layer = 6
MESH = pl.DeviceIdType.MESH
HIGHEST = lax.Precision.HIGHEST
ROW = 8
CH = 4


def split_coeff(value):
    high = float(ml_dtypes.bfloat16(value))
    low = float(ml_dtypes.bfloat16(value - high))
    return high, low


def fill_band(ref, part):
    size = ref.shape[0]
    rows = lax.broadcasted_iota(jnp.int32, ref.shape, 0)
    cols = lax.broadcasted_iota(jnp.int32, ref.shape, 1)
    far = jnp.abs(rows - cols)
    band = jnp.zeros(ref.shape, jnp.float32)
    for j in range(1, 5):
        band = jnp.where(far == j, split_coeff(coeffs[j])[part], band)
    ref[...] = band.astype(jnp.bfloat16)


def kernel(
    n_gx,
    n_shot,
    code_hbm,
    assign_hbm,
    px_hbm,
    py_hbm,
    wav_hbm,
    speed_hbm,
    press_hbm,
    prev_hbm,
    traces_hbm,
    out_hbm,
    misfit_hbm,
    code_ref,
    assign_ref,
    px_ref,
    py_ref,
    wav_ref,
    field,
    speed,
    traces,
    obs,
    obs_send,
    obs_recv,
    pack,
    pack_recv,
    sources,
    record,
    record_in,
    misfit,
    band_hi,
    band_lo,
    x_send,
    x_recv,
    z_send,
    z_recv,
    load_sem,
    swap_send,
    swap_recv,
    traces_sem,
    small_sem,
    init_send,
    pack_send,
    pack_rsem,
    obs_ssem,
    obs_rsem,
    rec_send,
    rec_recv,
    out_sem,
    out_send,
    out_recv,
    mis_sem,
):
    gx = lax.axis_index("gx")
    core = lax.axis_index("gy")
    shot = lax.axis_index("shot")
    depth = speed_hbm.shape[0]
    half = depth // 2
    wide = speed_hbm.shape[1]
    steps = record.shape[1]
    nsh = code_ref.shape[0]
    last = steps % 2
    rest = 1 - last
    nchunk = half // CH
    own = pl.ds(ROW, wide)
    has_left = gx > 0
    has_right = gx < n_gx - 1
    other = 1 - core

    def shot_at(d):
        return lax.rem(shot + d, n_shot)

    def x_copy(slot, side, chunk):
        z = pl.ds(4 + CH * chunk, CH)
        if side == 0:
            src, dst, to = pl.ds(ROW, 4), pl.ds(ROW + wide, 4), gx - 1
        else:
            src, dst, to = pl.ds(ROW + wide - 4, 4), pl.ds(ROW - 4, 4), gx + 1
        return pltpu.make_async_remote_copy(
            src_ref=field.at[slot, :, z, src, :],
            dst_ref=field.at[slot, :, z, dst, :],
            send_sem=x_send.at[slot, side, chunk],
            recv_sem=x_recv.at[slot, side, chunk],
            device_id={"gx": to},
            device_id_type=MESH,
        )

    def z_copy(slot):
        src = jnp.where(core == 0, half, 4)
        dst = jnp.where(core == 0, 0, 4 + half)
        return pltpu.make_async_remote_copy(
            src_ref=field.at[slot, :, pl.ds(src, 4), own, :],
            dst_ref=field.at[slot, :, pl.ds(dst, 4), own, :],
            send_sem=z_send.at[slot],
            recv_sem=z_recv.at[slot],
            device_id={"gy": other},
            device_id_type=MESH,
        )

    def start_x(slot, chunk):
        @pl.when(has_left)
        def _():
            x_copy(slot, 0, chunk).start()

        @pl.when(has_right)
        def _():
            x_copy(slot, 1, chunk).start()

    def wait_x_recv(slot, chunk):
        @pl.when(has_right)
        def _():
            x_copy(slot, 0, chunk).wait_recv()

        @pl.when(has_left)
        def _():
            x_copy(slot, 1, chunk).wait_recv()

    def wait_x_send(slot, chunk):
        @pl.when(has_left)
        def _():
            x_copy(slot, 0, chunk).wait_send()

        @pl.when(has_right)
        def _():
            x_copy(slot, 1, chunk).wait_send()

    def place_of(which, to):
        if which == 0:
            src = press_hbm.at[0, pl.ds(to * (half - 4), half + 4)]
            return src, field.at[0, core, pl.ds(4 * (1 - to), half + 4), own, :]
        if which == 1:
            return speed_hbm.at[pl.ds(to * half, half)], speed.at[core]
        src = prev_hbm.at[0, pl.ds(to * half, half)]
        return src, field.at[1, core, pl.ds(4, half), own, :]

    def load(which):
        src, dst = place_of(which, core)
        return pltpu.make_async_copy(src, dst, load_sem.at[which])

    def swap(which):
        src, dst = place_of(which, other)
        return pltpu.make_async_remote_copy(
            src_ref=src,
            dst_ref=dst,
            send_sem=swap_send.at[which],
            recv_sem=swap_recv.at[which],
            device_id={"gy": other},
            device_id_type=MESH,
        )

    def init_copy(side, to, chunk):
        if side == 0:
            src, dst, nb = pl.ds(0, 4), pl.ds(ROW + wide, 4), gx - 1
        else:
            src, dst, nb = pl.ds(wide - 4, 4), pl.ds(ROW - 4, 4), gx + 1
        index = jnp.where(to == 0, nchunk - 1 - chunk, chunk)
        return pltpu.make_async_remote_copy(
            src_ref=press_hbm.at[0, pl.ds(to * half + CH * index, CH), src, :],
            dst_ref=field.at[0, core, pl.ds(4 + CH * index, CH), dst, :],
            send_sem=init_send.at[side, jnp.where(to == core, 0, 1), chunk],
            recv_sem=x_recv.at[0, side, index],
            device_id={"gx": nb, "gy": to},
            device_id_type=MESH,
        )

    def each_init(act):
        for chunk in range(nchunk):
            for to in (core, other):

                @pl.when(has_left)
                def _(chunk=chunk, to=to):
                    act(init_copy(0, to, chunk))

                @pl.when(has_right)
                def _(chunk=chunk, to=to):
                    act(init_copy(1, to, chunk))

    def out_copy(chunk):
        return pltpu.make_async_copy(
            field.at[last, core, pl.ds(4 + CH * chunk, CH), own, :],
            out_hbm.at[0, pl.ds(core * half + CH * chunk, CH)],
            out_sem.at[chunk],
        )

    def out_away(chunk):
        return pltpu.make_async_remote_copy(
            src_ref=field.at[last, other, pl.ds(4 + CH * chunk, CH), own, :],
            dst_ref=out_hbm.at[0, pl.ds(core * half + CH * chunk, CH)],
            send_sem=out_send.at[chunk],
            recv_sem=out_recv.at[chunk],
            device_id={"gy": other},
            device_id_type=MESH,
        )

    def rec_copy(which):
        rows = pl.ds(0, steps - 1) if which == 0 else pl.ds(steps - 1, 1)
        return pltpu.make_async_remote_copy(
            src_ref=record.at[1, rows],
            dst_ref=record_in.at[rows],
            send_sem=rec_send.at[which],
            recv_sem=rec_recv.at[which],
            device_id={"gy": other},
            device_id_type=MESH,
        )

    def pack_copy(d):
        return pltpu.make_async_remote_copy(
            src_ref=pack,
            dst_ref=pack_recv.at[d - 1],
            send_sem=pack_send.at[d - 1],
            recv_sem=pack_rsem.at[d - 1],
            device_id={"shot": shot_at(d)},
            device_id_type=MESH,
        )

    def obs_copy(d):
        return pltpu.make_async_remote_copy(
            src_ref=obs_send.at[d - 1],
            dst_ref=obs_recv.at[d - 1],
            send_sem=obs_ssem.at[d - 1],
            recv_sem=obs_rsem.at[d - 1],
            device_id={"shot": shot_at(d)},
            device_id_type=MESH,
        )

    barrier = pltpu.get_barrier_semaphore()

    def greet(device):
        pl.semaphore_signal(barrier, inc=1, device_id=device, device_id_type=MESH)

    @pl.when(has_left)
    def _():
        for to in (core, other):
            greet({"gx": gx - 1, "gy": to})

    @pl.when(has_right)
    def _():
        for to in (core, other):
            greet({"gx": gx + 1, "gy": to})

    greet({"gy": other})
    for d in range(1, n_shot):
        greet({"shot": shot_at(d)})

    small = [
        pltpu.make_async_copy(src, dst, small_sem.at[i])
        for i, (src, dst) in enumerate(
            (
                (code_hbm, code_ref),
                (assign_hbm, assign_ref),
                (px_hbm, px_ref),
                (py_hbm, py_ref),
                (wav_hbm, wav_ref),
            )
        )
    ]
    for copy in small:
        copy.start()
    for which in range(3):
        load(which).start()
    traces_in = pltpu.make_async_copy(traces_hbm, traces, traces_sem)
    traces_in.start()

    for slot in range(2):
        for h in range(2):

            @pl.when(jnp.logical_not(has_left))
            def _(slot=slot, h=h):
                field[slot, h, :, 0:ROW, :] = jnp.zeros((half + 8, ROW, 128), jnp.float32)

            @pl.when(jnp.logical_not(has_right))
            def _(slot=slot, h=h):
                field[slot, h, :, ROW + wide :, :] = jnp.zeros((half + 8, 8, 128), jnp.float32)

            field[slot, h, pl.ds(core * (half + 4), 4), own, :] = jnp.zeros(
                (4, wide, 128), jnp.float32
            )

    fill_band(band_hi, 0)
    fill_band(band_lo, 1)

    greeted = n_shot + 2 * (has_left.astype(jnp.int32) + has_right.astype(jnp.int32))
    pl.semaphore_wait(barrier, greeted)
    swap(0).start()
    each_init(lambda copy: copy.start())
    for which in (1, 2):
        swap(which).start()

    def read_signs():
        return [(2 * code_ref[k] - 1).astype(jnp.float32) for k in range(nsh)]

    def send_pack():
        for copy in small:
            copy.wait()

        lane = lax.broadcasted_iota(jnp.int32, (1, 128), 1)
        lane8 = lax.broadcasted_iota(jnp.int32, (nsh, 128), 1)
        sub8 = lax.broadcasted_iota(jnp.int32, (nsh, 128), 0)
        rows3 = [jnp.zeros((1, 128), jnp.int32) for _ in range(3)]
        signed = jnp.zeros((nsh, 128), jnp.float32)
        signs = read_signs()
        for s in range(nsh):
            mine = lane == shot * nsh + s
            for r, ref in enumerate((assign_ref, px_ref, py_ref)):
                rows3[r] = jnp.where(mine, ref[s], rows3[r])
            signed = jnp.where((lane8 == shot * nsh + s) & (sub8 == s), signs[s], signed)
        pack[0:steps, :] = lax.dot_general(
            wav_ref[...], signed, (((0,), (0,)), ((), ())), precision=HIGHEST,
            preferred_element_type=jnp.float32,
        )
        for r in range(3):
            pack[steps + r : steps + r + 1, :] = rows3[r].astype(jnp.float32)
        pack[steps + 3 :, :] = jnp.zeros((pack.shape[0] - steps - 3, 128), jnp.float32)
        for d in range(1, n_shot):
            pack_copy(d).start()

    def chunk_of(i):
        return jnp.where(core == 0, nchunk - 1 - i, i)

    def encode_rows(first, count):
        signs = read_signs()
        scales = [
            [jnp.where(assign_ref[k] == shot_at(d), signs[k], 0.0) for k in range(nsh)]
            for d in range(n_shot)
        ]
        for r in range(count):
            t = first + r
            rows = [traces[k, t] for k in range(nsh)]
            for d in range(n_shot):
                total = scales[d][0] * rows[0]
                for k in range(1, nsh):
                    total += scales[d][k] * rows[k]
                if d == 0:
                    obs[t] = total
                else:
                    obs_send[d - 1, t] = total

    for which in range(3):
        load(which).wait()
        swap(which).wait_recv()

    def make_sources():
        table = pack[...]
        for d in range(1, n_shot):
            table = table + pack_recv[d - 1]
        weight = jnp.where(
            table[steps : steps + 1] == shot.astype(jnp.float32), table[0:steps], 0.0
        )
        local_x = table[steps + 1 : steps + 2] - (gx * wide).astype(jnp.float32)
        onex = jnp.where(
            local_x == lax.broadcasted_iota(jnp.int32, (wide, 128), 0).astype(jnp.float32), 1.0, 0.0
        )
        oney = jnp.where(
            table[steps + 2 : steps + 3]
            == lax.broadcasted_iota(jnp.int32, (256, 128), 0).astype(jnp.float32),
            1.0,
            0.0,
        )
        left = (weight[:, None, :] * onex[None]).reshape(steps * wide, 128)
        grid = lax.dot_general(
            left, oney, (((1,), (1,)), ((), ())), precision=HIGHEST,
            preferred_element_type=jnp.float32,
        )
        for h in range(2):
            sources[h] = grid[:, 128 * h : 128 * (h + 1)].reshape(steps, wide, 128)

    def one_chunk(n, i):
        now = lax.rem(n, 2)
        new = 1 - now
        chunk = chunk_of(i)
        z0 = 4 + CH * chunk
        zs = pl.ds(z0, CH)
        if i == 0:

            @pl.when(n > 0)
            def _():
                z_copy(now).wait_recv()

            @pl.when(n > 1)
            def _():
                z_copy(new).wait_send()

        center = [field[now, h, zs, own, :] for h in range(2)]
        both = jnp.concatenate([v.reshape(CH * wide, 128) for v in center], axis=1)
        hi = both.astype(jnp.bfloat16)
        lo = (both - hi.astype(jnp.float32)).astype(jnp.bfloat16)
        dot = functools.partial(jnp.dot, preferred_element_type=jnp.float32)
        along_y = dot(hi, band_hi[...]) + dot(lo, band_hi[...]) + dot(hi, band_lo[...])
        totals = []
        for h in range(2):
            total = along_y[:, 128 * h : 128 * (h + 1)].reshape(CH, wide, 128)
            total = total + (3.0 * coeffs[0]) * center[h]
            for j in range(1, 5):
                total = total + coeffs[j] * (
                    field[now, h, pl.ds(z0 + j, CH), own, :]
                    + field[now, h, pl.ds(z0 - j, CH), own, :]
                )
            totals.append(total)

        if i == nchunk - 1:

            @pl.when(n == 0)
            def _():
                for d in range(1, n_shot):
                    pack_copy(d).wait_recv()

                @pl.when(core == 0)
                def _():
                    make_sources()

        @pl.when(n > 1)
        def _():
            wait_x_send(new, chunk)

        wait_x_recv(now, chunk)

        for h in range(2):
            total = totals[h]
            for j in range(1, 5):
                total = total + coeffs[j] * (
                    field[now, h, zs, pl.ds(ROW + j, wide), :]
                    + field[now, h, zs, pl.ds(ROW - j, wide), :]
                )
            field[new, h, zs, own, :] = (
                2.0 * field[now, h, zs, own, :] - field[new, h, zs, own, :]
                + speed[h, pl.ds(CH * chunk, CH)] * total
            )

        @pl.when((core == 0) & (chunk == 0))
        def _():
            for h in range(2):
                at = 4 + source_layer
                field[new, h, at, own, :] = field[new, h, at, own, :] + sources[h, n]
                record[h, n] = field[new, h, 4 + record_layer, own, :]

        @pl.when(n < steps - 1)
        def _():
            if i == 0:
                z_copy(new).start()
            start_x(new, chunk)

        if i == 0:

            @pl.when(n == 0)
            def _():
                send_pack()

        @pl.when(n == steps - 1)
        def _():
            out_away(chunk).start()
            out_copy(chunk).start()

    batch = 2
    encoding = -(-steps // batch)

    def one_step(n, carry):
        for i in range(nchunk):
            one_chunk(n, i)

        @pl.when(n < encoding)
        def _():
            pl.when(n == 0)(traces_in.wait)
            encode_rows(n * batch, batch)

        @pl.when(n == encoding)
        def _():
            for d in range(1, n_shot):
                obs_copy(d).start()

        @pl.when((n == steps - 2) & (core == 0))
        def _():
            rec_copy(0).start()

        return carry

    lax.fori_loop(0, steps, one_step, 0)

    @pl.when(core == 0)
    def _():
        rec_copy(1).start()

    def mis_copy(which):
        rows = pl.ds(0, steps - 1) if which == 0 else pl.ds(steps - 1, 1)
        return pltpu.make_async_copy(
            misfit.at[rows], misfit_hbm.at[0, rows], mis_sem.at[which]
        )

    for d in range(1, n_shot):
        obs_copy(d).wait_recv()
    for which in range(2):
        rows = pl.ds(0, steps - 1) if which == 0 else pl.ds(steps - 1, 1)
        observed = obs[rows]
        for d in range(1, n_shot):
            observed = observed + obs_recv[d - 1, rows]

        @pl.when(core == 0)
        def _(rows=rows, observed=observed):
            misfit[rows] = record[0, rows] - observed

        @pl.when(core == 1)
        def _(which=which, rows=rows, observed=observed):
            rec_copy(which).wait_recv()
            misfit[rows] = record_in[rows] - observed

        mis_copy(which).start()

    z_copy(rest).wait_send()
    for i in range(nchunk):
        wait_x_send(rest, i)
    for which in range(3):
        swap(which).wait_send()
    for d in range(1, n_shot):
        pack_copy(d).wait_send()
        obs_copy(d).wait_send()

    @pl.when(core == 0)
    def _():
        rec_copy(0).wait_send()
        rec_copy(1).wait_send()

    each_init(lambda copy: copy.wait_send())
    for chunk in range(nchunk):
        out_copy(chunk).wait()
        out_away(chunk).wait()
    for which in range(2):
        mis_copy(which).wait()


def copy_kernel(a_in, b_in, a_out, b_out, a_mid, b_mid, sem_in, sem_out):
    pieces = []
    for src, mid, dst, count in ((a_in, a_mid, a_out, 4), (b_in, b_mid, b_out, 2)):
        size = src.shape[1] // count
        for i in range(count):
            rows = pl.ds(i * size, size)
            at = len(pieces)
            pieces.append(
                (
                    pltpu.make_async_copy(src.at[0, rows], mid.at[rows], sem_in.at[at]),
                    pltpu.make_async_copy(mid.at[rows], dst.at[0, rows], sem_out.at[at]),
                )
            )
    for first, _ in pieces:
        first.start()
    for first, second in pieces:
        first.wait()
        second.start()
    for _, second in pieces:
        second.wait()


def on_device(n_gx, n_shot, speed, pressure, previous, wavelets, traces, code, assign, px, py):
    depth, wide, wide_y = speed.shape
    nsh, steps = wavelets.shape
    half = depth // 2
    pairs = max(n_shot - 1, 1)
    f32 = jnp.float32
    hbm = pl.BlockSpec(memory_space=pltpu.HBM)
    dma = pltpu.SemaphoreType.DMA
    nchunk = half // CH
    shapes = (
        jax.ShapeDtypeStruct((1, depth, wide, wide_y), f32),
        jax.ShapeDtypeStruct((1, steps, wide, wide_y), f32),
    )
    results = pl.pallas_call(
        functools.partial(kernel, n_gx, n_shot),
        out_shape=shapes,
        in_specs=[hbm] * 9,
        out_specs=(hbm, hbm),
        scratch_shapes=[
            pltpu.SMEM((nsh,), jnp.int32),
            pltpu.SMEM((nsh,), jnp.int32),
            pltpu.SMEM((nsh,), jnp.int32),
            pltpu.SMEM((nsh,), jnp.int32),
            pltpu.VMEM((nsh, steps), f32),
            pltpu.VMEM((2, 2, half + 8, wide + 16, wide_y), f32),
            pltpu.VMEM((2, half, wide, wide_y), f32),
            pltpu.VMEM((nsh, steps, wide, wide_y), f32),
            pltpu.VMEM((steps, wide, wide_y), f32),
            pltpu.VMEM((pairs, steps, wide, wide_y), f32),
            pltpu.VMEM((pairs, steps, wide, wide_y), f32),
            pltpu.VMEM((-(-(steps + 3) // 8) * 8, 128), f32),
            pltpu.VMEM((pairs, -(-(steps + 3) // 8) * 8, 128), f32),
            pltpu.VMEM((2, steps, wide, wide_y), f32),
            pltpu.VMEM((2, steps, wide, wide_y), f32),
            pltpu.VMEM((steps, wide, wide_y), f32),
            pltpu.VMEM((steps, wide, wide_y), f32),
            pltpu.VMEM((2 * wide_y, 2 * wide_y), jnp.bfloat16),
            pltpu.VMEM((2 * wide_y, 2 * wide_y), jnp.bfloat16),
            dma((2, 2, nchunk)),
            dma((2, 2, nchunk)),
            dma((2,)),
            dma((2,)),
            dma((3,)),
            dma((3,)),
            dma((3,)),
            dma,
            dma((5,)),
            dma((2, 2, nchunk)),
            dma((pairs,)),
            dma((pairs,)),
            dma((pairs,)),
            dma((pairs,)),
            dma((2,)),
            dma((2,)),
            dma((nchunk,)),
            dma((nchunk,)),
            dma((nchunk,)),
            dma((2,)),
        ],
        compiler_params=pltpu.CompilerParams(
            collective_id=0, has_side_effects=True, vmem_limit_bytes=62 * 1024 * 1024
        ),
    )(code, assign, px, py, wavelets, speed, pressure, previous, traces)
    return pl.pallas_call(
        copy_kernel,
        out_shape=shapes,
        in_specs=[hbm] * 2,
        out_specs=(hbm, hbm),
        scratch_shapes=[
            pltpu.VMEM((depth, wide, wide_y), f32),
            pltpu.VMEM((steps, wide, wide_y), f32),
            dma((6,)),
            dma((6,)),
        ],
        compiler_params=pltpu.CompilerParams(vmem_limit_bytes=62 * 1024 * 1024),
    )(*results)


def solution(mesh):
    return jax.shard_map(
        functools.partial(on_device, mesh.shape["gx"], mesh.shape["shot"]),
        mesh=mesh,
        in_specs=(
            P("grp", "gx", "gy"),
            P(("grp", "shot"), None, "gx", "gy"),
            P(("grp", "shot"), None, "gx", "gy"),
            P(("grp", "shot"), None),
            P(("grp", "shot"), None, "gx", "gy"),
            P(("grp", "shot")),
            P(("grp", "shot")),
            P(("grp", "shot")),
            P(("grp", "shot")),
        ),
        out_specs=(P(("grp", "shot"), None, "gx", "gy"), P(("grp", "shot"), None, "gx", "gy")),
        check_vma=False,
    )
```

```python
import functools

import jax
import jax.numpy as jnp
import ml_dtypes
from jax import lax
from jax.experimental import pallas as pl
from jax.experimental.pallas import tpu as pltpu
from jax.sharding import PartitionSpec as P

coeffs = (-205.0 / 72.0, 8.0 / 5.0, -1.0 / 5.0, 8.0 / 315.0, -1.0 / 560.0)
source_layer = 2
record_layer = 6
MESH = pl.DeviceIdType.MESH
HIGHEST = lax.Precision.HIGHEST
ROW = 8
CH = 4


def split_coeff(value):
    high = float(ml_dtypes.bfloat16(value))
    low = float(ml_dtypes.bfloat16(value - high))
    return high, low


def fill_band(ref, part):
    size = ref.shape[0]
    rows = lax.broadcasted_iota(jnp.int32, ref.shape, 0)
    cols = lax.broadcasted_iota(jnp.int32, ref.shape, 1)
    far = jnp.abs(rows - cols)
    band = jnp.zeros(ref.shape, jnp.float32)
    for j in range(1, 5):
        band = jnp.where(far == j, split_coeff(coeffs[j])[part], band)
    ref[...] = band.astype(jnp.bfloat16)


def kernel(
    n_gx,
    n_shot,
    code_hbm,
    assign_hbm,
    px_hbm,
    py_hbm,
    wav_hbm,
    speed_hbm,
    press_hbm,
    prev_hbm,
    traces_hbm,
    out_hbm,
    misfit_hbm,
    code_ref,
    assign_ref,
    px_ref,
    py_ref,
    wav_ref,
    field,
    speed,
    traces,
    obs,
    obs_send,
    obs_recv,
    pack,
    pack_recv,
    sources,
    record,
    record_in,
    misfit,
    band_hi,
    band_lo,
    x_send,
    x_recv,
    z_send,
    z_recv,
    load_sem,
    swap_send,
    swap_recv,
    traces_sem,
    small_sem,
    init_send,
    pack_send,
    pack_rsem,
    obs_ssem,
    obs_rsem,
    rec_send,
    rec_recv,
    out_sem,
    out_send,
    out_recv,
    mis_sem,
):
    gx = lax.axis_index("gx")
    core = lax.axis_index("gy")
    shot = lax.axis_index("shot")
    depth = speed_hbm.shape[0]
    half = depth // 2
    wide = speed_hbm.shape[1]
    steps = record.shape[1]
    nsh = code_ref.shape[0]
    last = steps % 2
    rest = 1 - last
    nchunk = half // CH
    own = pl.ds(ROW, wide)
    has_left = gx > 0
    has_right = gx < n_gx - 1
    other = 1 - core

    def shot_at(d):
        return lax.rem(shot + d, n_shot)

    def x_copy(slot, side, chunk):
        z = pl.ds(4 + CH * chunk, CH)
        if side == 0:
            src, dst, to = pl.ds(ROW, 4), pl.ds(ROW + wide, 4), gx - 1
        else:
            src, dst, to = pl.ds(ROW + wide - 4, 4), pl.ds(ROW - 4, 4), gx + 1
        return pltpu.make_async_remote_copy(
            src_ref=field.at[slot, :, z, src, :],
            dst_ref=field.at[slot, :, z, dst, :],
            send_sem=x_send.at[slot, side, chunk],
            recv_sem=x_recv.at[slot, side, chunk],
            device_id={"gx": to},
            device_id_type=MESH,
        )

    def z_copy(slot):
        src = jnp.where(core == 0, half, 4)
        dst = jnp.where(core == 0, 0, 4 + half)
        return pltpu.make_async_remote_copy(
            src_ref=field.at[slot, :, pl.ds(src, 4), own, :],
            dst_ref=field.at[slot, :, pl.ds(dst, 4), own, :],
            send_sem=z_send.at[slot],
            recv_sem=z_recv.at[slot],
            device_id={"gy": other},
            device_id_type=MESH,
        )

    def start_x(slot, chunk):
        @pl.when(has_left)
        def _():
            x_copy(slot, 0, chunk).start()

        @pl.when(has_right)
        def _():
            x_copy(slot, 1, chunk).start()

    def wait_x_recv(slot, chunk):
        @pl.when(has_right)
        def _():
            x_copy(slot, 0, chunk).wait_recv()

        @pl.when(has_left)
        def _():
            x_copy(slot, 1, chunk).wait_recv()

    def wait_x_send(slot, chunk):
        @pl.when(has_left)
        def _():
            x_copy(slot, 0, chunk).wait_send()

        @pl.when(has_right)
        def _():
            x_copy(slot, 1, chunk).wait_send()

    def place_of(which, to):
        if which == 0:
            src = press_hbm.at[0, pl.ds(to * (half - 4), half + 4)]
            return src, field.at[0, core, pl.ds(4 * (1 - to), half + 4), own, :]
        if which == 1:
            return speed_hbm.at[pl.ds(to * half, half)], speed.at[core]
        src = prev_hbm.at[0, pl.ds(to * half, half)]
        return src, field.at[1, core, pl.ds(4, half), own, :]

    def load(which):
        src, dst = place_of(which, core)
        return pltpu.make_async_copy(src, dst, load_sem.at[which])

    def swap(which):
        src, dst = place_of(which, other)
        return pltpu.make_async_remote_copy(
            src_ref=src,
            dst_ref=dst,
            send_sem=swap_send.at[which],
            recv_sem=swap_recv.at[which],
            device_id={"gy": other},
            device_id_type=MESH,
        )

    def init_copy(side, to, chunk):
        if side == 0:
            src, dst, nb = pl.ds(0, 4), pl.ds(ROW + wide, 4), gx - 1
        else:
            src, dst, nb = pl.ds(wide - 4, 4), pl.ds(ROW - 4, 4), gx + 1
        index = jnp.where(to == 0, nchunk - 1 - chunk, chunk)
        return pltpu.make_async_remote_copy(
            src_ref=press_hbm.at[0, pl.ds(to * half + CH * index, CH), src, :],
            dst_ref=field.at[0, core, pl.ds(4 + CH * index, CH), dst, :],
            send_sem=init_send.at[side, jnp.where(to == core, 0, 1), chunk],
            recv_sem=x_recv.at[0, side, index],
            device_id={"gx": nb, "gy": to},
            device_id_type=MESH,
        )

    def each_init(act):
        for chunk in range(nchunk):
            for to in (core, other):

                @pl.when(has_left)
                def _(chunk=chunk, to=to):
                    act(init_copy(0, to, chunk))

                @pl.when(has_right)
                def _(chunk=chunk, to=to):
                    act(init_copy(1, to, chunk))

    def out_copy(chunk):
        return pltpu.make_async_copy(
            field.at[last, core, pl.ds(4 + CH * chunk, CH), own, :],
            out_hbm.at[0, pl.ds(core * half + CH * chunk, CH)],
            out_sem.at[chunk],
        )

    def out_away(chunk):
        return pltpu.make_async_remote_copy(
            src_ref=field.at[last, other, pl.ds(4 + CH * chunk, CH), own, :],
            dst_ref=out_hbm.at[0, pl.ds(core * half + CH * chunk, CH)],
            send_sem=out_send.at[chunk],
            recv_sem=out_recv.at[chunk],
            device_id={"gy": other},
            device_id_type=MESH,
        )

    def rec_copy(which):
        rows = pl.ds(0, steps - 1) if which == 0 else pl.ds(steps - 1, 1)
        return pltpu.make_async_remote_copy(
            src_ref=record.at[1, rows],
            dst_ref=record_in.at[rows],
            send_sem=rec_send.at[which],
            recv_sem=rec_recv.at[which],
            device_id={"gy": other},
            device_id_type=MESH,
        )

    def pack_copy(d):
        return pltpu.make_async_remote_copy(
            src_ref=pack,
            dst_ref=pack_recv.at[d - 1],
            send_sem=pack_send.at[d - 1],
            recv_sem=pack_rsem.at[d - 1],
            device_id={"shot": shot_at(d)},
            device_id_type=MESH,
        )

    def obs_copy(d):
        return pltpu.make_async_remote_copy(
            src_ref=obs_send.at[d - 1],
            dst_ref=obs_recv.at[d - 1],
            send_sem=obs_ssem.at[d - 1],
            recv_sem=obs_rsem.at[d - 1],
            device_id={"shot": shot_at(d)},
            device_id_type=MESH,
        )

    barrier = pltpu.get_barrier_semaphore()

    def greet(device):
        pl.semaphore_signal(barrier, inc=1, device_id=device, device_id_type=MESH)

    @pl.when(has_left)
    def _():
        for to in (core, other):
            greet({"gx": gx - 1, "gy": to})

    @pl.when(has_right)
    def _():
        for to in (core, other):
            greet({"gx": gx + 1, "gy": to})

    greet({"gy": other})
    for d in range(1, n_shot):
        greet({"shot": shot_at(d)})

    small = [
        pltpu.make_async_copy(src, dst, small_sem.at[i])
        for i, (src, dst) in enumerate(
            (
                (code_hbm, code_ref),
                (assign_hbm, assign_ref),
                (px_hbm, px_ref),
                (py_hbm, py_ref),
                (wav_hbm, wav_ref),
            )
        )
    ]
    for copy in small:
        copy.start()
    for which in range(3):
        load(which).start()
    traces_in = pltpu.make_async_copy(traces_hbm, traces, traces_sem)
    traces_in.start()

    for slot in range(2):
        for h in range(2):

            @pl.when(jnp.logical_not(has_left))
            def _(slot=slot, h=h):
                field[slot, h, :, 0:ROW, :] = jnp.zeros((half + 8, ROW, 128), jnp.float32)

            @pl.when(jnp.logical_not(has_right))
            def _(slot=slot, h=h):
                field[slot, h, :, ROW + wide :, :] = jnp.zeros((half + 8, 8, 128), jnp.float32)

            field[slot, h, pl.ds(core * (half + 4), 4), own, :] = jnp.zeros(
                (4, wide, 128), jnp.float32
            )

    fill_band(band_hi, 0)
    fill_band(band_lo, 1)

    greeted = n_shot + 2 * (has_left.astype(jnp.int32) + has_right.astype(jnp.int32))
    pl.semaphore_wait(barrier, greeted)
    swap(0).start()
    each_init(lambda copy: copy.start())
    for which in (1, 2):
        swap(which).start()

    def read_signs():
        return [(2 * code_ref[k] - 1).astype(jnp.float32) for k in range(nsh)]

    def send_pack():

        lane = lax.broadcasted_iota(jnp.int32, (1, 128), 1)
        lane8 = lax.broadcasted_iota(jnp.int32, (nsh, 128), 1)
        sub8 = lax.broadcasted_iota(jnp.int32, (nsh, 128), 0)
        rows3 = [jnp.zeros((1, 128), jnp.int32) for _ in range(3)]
        signed = jnp.zeros((nsh, 128), jnp.float32)
        signs = read_signs()
        for s in range(nsh):
            mine = lane == shot * nsh + s
            for r, ref in enumerate((assign_ref, px_ref, py_ref)):
                rows3[r] = jnp.where(mine, ref[s], rows3[r])
            signed = jnp.where((lane8 == shot * nsh + s) & (sub8 == s), signs[s], signed)
        pack[0:steps, :] = lax.dot_general(
            wav_ref[...], signed, (((0,), (0,)), ((), ())), precision=HIGHEST,
            preferred_element_type=jnp.float32,
        )
        for r in range(3):
            pack[steps + r : steps + r + 1, :] = rows3[r].astype(jnp.float32)
        pack[steps + 3 :, :] = jnp.zeros((pack.shape[0] - steps - 3, 128), jnp.float32)
        for d in range(1, n_shot):
            pack_copy(d).start()

    def chunk_of(i):
        return jnp.where(core == 0, nchunk - 1 - i, i)

    def encode_rows(first, count):
        signs = read_signs()
        scales = [
            [jnp.where(assign_ref[k] == shot_at(d), signs[k], 0.0) for k in range(nsh)]
            for d in range(n_shot)
        ]
        for r in range(count):
            t = first + r
            rows = [traces[k, t] for k in range(nsh)]
            for d in range(n_shot):
                total = scales[d][0] * rows[0]
                for k in range(1, nsh):
                    total += scales[d][k] * rows[k]
                if d == 0:
                    obs[t] = total
                else:
                    obs_send[d - 1, t] = total

    for copy in small:
        copy.wait()
    traces_in.wait()

    def encode_pair(pair, carry):
        encode_rows(2 * pair, 2)
        return carry

    lax.fori_loop(0, steps // 2, encode_pair, 0)
    for d in range(1, n_shot):
        obs_copy(d).start()
    for which in range(3):
        load(which).wait()
        swap(which).wait_recv()

    def make_sources():
        table = pack[...]
        for d in range(1, n_shot):
            table = table + pack_recv[d - 1]
        weight = jnp.where(
            table[steps : steps + 1] == shot.astype(jnp.float32), table[0:steps], 0.0
        )
        local_x = table[steps + 1 : steps + 2] - (gx * wide).astype(jnp.float32)
        onex = jnp.where(
            local_x == lax.broadcasted_iota(jnp.int32, (wide, 128), 0).astype(jnp.float32), 1.0, 0.0
        )
        oney = jnp.where(
            table[steps + 2 : steps + 3]
            == lax.broadcasted_iota(jnp.int32, (256, 128), 0).astype(jnp.float32),
            1.0,
            0.0,
        )
        left = (weight[:, None, :] * onex[None]).reshape(steps * wide, 128)
        grid = lax.dot_general(
            left, oney, (((1,), (1,)), ((), ())), precision=HIGHEST,
            preferred_element_type=jnp.float32,
        )
        for h in range(2):
            sources[h] = grid[:, 128 * h : 128 * (h + 1)].reshape(steps, wide, 128)

    def one_chunk(n, i):
        now = lax.rem(n, 2)
        new = 1 - now
        chunk = chunk_of(i)
        z0 = 4 + CH * chunk
        zs = pl.ds(z0, CH)
        if i == 0:

            @pl.when(n > 0)
            def _():
                z_copy(now).wait_recv()

            @pl.when(n > 1)
            def _():
                z_copy(new).wait_send()

        center = [field[now, h, zs, own, :] for h in range(2)]
        both = jnp.concatenate([v.reshape(CH * wide, 128) for v in center], axis=1)
        hi = both.astype(jnp.bfloat16)
        lo = (both - hi.astype(jnp.float32)).astype(jnp.bfloat16)
        dot = functools.partial(jnp.dot, preferred_element_type=jnp.float32)
        parts = dot(jnp.concatenate([hi, lo], axis=0), band_hi[...])
        along_y = parts[: CH * wide] + parts[CH * wide :] + dot(hi, band_lo[...])
        totals = []
        for h in range(2):
            total = along_y[:, 128 * h : 128 * (h + 1)].reshape(CH, wide, 128)
            total = total + (3.0 * coeffs[0]) * center[h]
            for j in range(1, 5):
                total = total + coeffs[j] * (
                    field[now, h, pl.ds(z0 + j, CH), own, :]
                    + field[now, h, pl.ds(z0 - j, CH), own, :]
                )
            totals.append(total)

        if i == nchunk - 1:

            @pl.when(n == 0)
            def _():
                for d in range(1, n_shot):
                    pack_copy(d).wait_recv()

                @pl.when(core == 0)
                def _():
                    make_sources()

        @pl.when(n > 1)
        def _():
            wait_x_send(new, chunk)

        wait_x_recv(now, chunk)

        for h in range(2):
            total = totals[h]
            for j in range(1, 5):
                total = total + coeffs[j] * (
                    field[now, h, zs, pl.ds(ROW + j, wide), :]
                    + field[now, h, zs, pl.ds(ROW - j, wide), :]
                )
            field[new, h, zs, own, :] = (
                2.0 * field[now, h, zs, own, :] - field[new, h, zs, own, :]
                + speed[h, pl.ds(CH * chunk, CH)] * total
            )

        @pl.when((core == 0) & (chunk == 0))
        def _():
            for h in range(2):
                at = 4 + source_layer
                field[new, h, at, own, :] = field[new, h, at, own, :] + sources[h, n]
                record[h, n] = field[new, h, 4 + record_layer, own, :]

        @pl.when(n < steps - 1)
        def _():
            if i == 0:
                z_copy(new).start()
            start_x(new, chunk)

        if i == 0:

            @pl.when(n == 0)
            def _():
                send_pack()

        @pl.when(n == steps - 1)
        def _():
            out_away(chunk).start()
            out_copy(chunk).start()

    def one_step(n, carry):
        for i in range(nchunk):
            one_chunk(n, i)

        @pl.when((n == steps - 2) & (core == 0))
        def _():
            rec_copy(0).start()

        return carry

    lax.fori_loop(0, steps, one_step, 0)

    @pl.when(core == 0)
    def _():
        rec_copy(1).start()

    def mis_copy(which):
        rows = pl.ds(0, steps - 1) if which == 0 else pl.ds(steps - 1, 1)
        return pltpu.make_async_copy(
            misfit.at[rows], misfit_hbm.at[0, rows], mis_sem.at[which]
        )

    for d in range(1, n_shot):
        obs_copy(d).wait_recv()
    for which in range(2):
        rows = pl.ds(0, steps - 1) if which == 0 else pl.ds(steps - 1, 1)
        observed = obs[rows]
        for d in range(1, n_shot):
            observed = observed + obs_recv[d - 1, rows]

        @pl.when(core == 0)
        def _(rows=rows, observed=observed):
            misfit[rows] = record[0, rows] - observed

        @pl.when(core == 1)
        def _(which=which, rows=rows, observed=observed):
            rec_copy(which).wait_recv()
            misfit[rows] = record_in[rows] - observed

        mis_copy(which).start()

    z_copy(rest).wait_send()
    for i in range(nchunk):
        wait_x_send(rest, i)
    for which in range(3):
        swap(which).wait_send()
    for d in range(1, n_shot):
        pack_copy(d).wait_send()
        obs_copy(d).wait_send()

    @pl.when(core == 0)
    def _():
        rec_copy(0).wait_send()
        rec_copy(1).wait_send()

    each_init(lambda copy: copy.wait_send())
    for chunk in range(nchunk):
        out_copy(chunk).wait()
        out_away(chunk).wait()
    for which in range(2):
        mis_copy(which).wait()


def copy_kernel(a_in, b_in, a_out, b_out, a_mid, b_mid, sem_in, sem_out):
    pieces = []
    for src, mid, dst, count in ((a_in, a_mid, a_out, 4), (b_in, b_mid, b_out, 2)):
        size = src.shape[1] // count
        for i in range(count):
            rows = pl.ds(i * size, size)
            at = len(pieces)
            pieces.append(
                (
                    pltpu.make_async_copy(src.at[0, rows], mid.at[rows], sem_in.at[at]),
                    pltpu.make_async_copy(mid.at[rows], dst.at[0, rows], sem_out.at[at]),
                )
            )
    for first, _ in pieces:
        first.start()
    for first, second in pieces:
        first.wait()
        second.start()
    for _, second in pieces:
        second.wait()


def on_device(n_gx, n_shot, speed, pressure, previous, wavelets, traces, code, assign, px, py):
    depth, wide, wide_y = speed.shape
    nsh, steps = wavelets.shape
    half = depth // 2
    pairs = max(n_shot - 1, 1)
    f32 = jnp.float32
    hbm = pl.BlockSpec(memory_space=pltpu.HBM)
    dma = pltpu.SemaphoreType.DMA
    nchunk = half // CH
    shapes = (
        jax.ShapeDtypeStruct((1, depth, wide, wide_y), f32),
        jax.ShapeDtypeStruct((1, steps, wide, wide_y), f32),
    )
    results = pl.pallas_call(
        functools.partial(kernel, n_gx, n_shot),
        out_shape=shapes,
        in_specs=[hbm] * 9,
        out_specs=(hbm, hbm),
        scratch_shapes=[
            pltpu.SMEM((nsh,), jnp.int32),
            pltpu.SMEM((nsh,), jnp.int32),
            pltpu.SMEM((nsh,), jnp.int32),
            pltpu.SMEM((nsh,), jnp.int32),
            pltpu.VMEM((nsh, steps), f32),
            pltpu.VMEM((2, 2, half + 8, wide + 16, wide_y), f32),
            pltpu.VMEM((2, half, wide, wide_y), f32),
            pltpu.VMEM((nsh, steps, wide, wide_y), f32),
            pltpu.VMEM((steps, wide, wide_y), f32),
            pltpu.VMEM((pairs, steps, wide, wide_y), f32),
            pltpu.VMEM((pairs, steps, wide, wide_y), f32),
            pltpu.VMEM((-(-(steps + 3) // 8) * 8, 128), f32),
            pltpu.VMEM((pairs, -(-(steps + 3) // 8) * 8, 128), f32),
            pltpu.VMEM((2, steps, wide, wide_y), f32),
            pltpu.VMEM((2, steps, wide, wide_y), f32),
            pltpu.VMEM((steps, wide, wide_y), f32),
            pltpu.VMEM((steps, wide, wide_y), f32),
            pltpu.VMEM((2 * wide_y, 2 * wide_y), jnp.bfloat16),
            pltpu.VMEM((2 * wide_y, 2 * wide_y), jnp.bfloat16),
            dma((2, 2, nchunk)),
            dma((2, 2, nchunk)),
            dma((2,)),
            dma((2,)),
            dma((3,)),
            dma((3,)),
            dma((3,)),
            dma,
            dma((5,)),
            dma((2, 2, nchunk)),
            dma((pairs,)),
            dma((pairs,)),
            dma((pairs,)),
            dma((pairs,)),
            dma((2,)),
            dma((2,)),
            dma((nchunk,)),
            dma((nchunk,)),
            dma((nchunk,)),
            dma((2,)),
        ],
        compiler_params=pltpu.CompilerParams(
            collective_id=0, has_side_effects=True, vmem_limit_bytes=62 * 1024 * 1024
        ),
    )(code, assign, px, py, wavelets, speed, pressure, previous, traces)
    return pl.pallas_call(
        copy_kernel,
        out_shape=shapes,
        in_specs=[hbm] * 2,
        out_specs=(hbm, hbm),
        scratch_shapes=[
            pltpu.VMEM((depth, wide, wide_y), f32),
            pltpu.VMEM((steps, wide, wide_y), f32),
            dma((6,)),
            dma((6,)),
        ],
        compiler_params=pltpu.CompilerParams(vmem_limit_bytes=62 * 1024 * 1024),
    )(*results)


def solution(mesh):
    return jax.shard_map(
        functools.partial(on_device, mesh.shape["gx"], mesh.shape["shot"]),
        mesh=mesh,
        in_specs=(
            P("grp", "gx", "gy"),
            P(("grp", "shot"), None, "gx", "gy"),
            P(("grp", "shot"), None, "gx", "gy"),
            P(("grp", "shot"), None),
            P(("grp", "shot"), None, "gx", "gy"),
            P(("grp", "shot")),
            P(("grp", "shot")),
            P(("grp", "shot")),
            P(("grp", "shot")),
        ),
        out_specs=(P(("grp", "shot"), None, "gx", "gy"), P(("grp", "shot"), None, "gx", "gy")),
        check_vma=False,
    )
```
